32 devices in a mesh: grp: 8 (over z, y), tp: 4 (over x, core).
Axes of the slice: x: 2, y: 2, z: 4, core: 2. Of those that a mesh axis runs over, the one named last changes fastest.
Arguments:
- hidden: bfloat16 [6144, 4608], P('grp', 'tp'), as said below
- norm_gain: float32 [4608], replicated, may hold values from 0.1 to 1.9
- q_weight: bfloat16 [4608, 2048], P(None, 'tp'), as said below
- k_weight: bfloat16 [4608, 1024], P(None, 'tp'), as said below
- v_weight: bfloat16 [4608, 1024], P(None, 'tp'), may hold values from -0.09375 to 0.09375
- kv_pages: bfloat16 [4096, 16, 8, 256], P('grp', None, 'tp'), as said below
- page_table: int32 [128, 256], P('grp'), may hold values from 0 to 527
- cache_len: int32 [128], P('grp'), may hold values from 1 to 4096, as said below
- tree_parent: int32 [128, 48], P('grp'), may hold values from -1 to 46, as said below
- accept_node: int32 [128], P('grp'), may hold values from 0 to 47
- pair_slot: int32 [8, 2], P('grp'), may hold values from 0 to 15, as said below
- far_len: int32 [8, 2], replicated, may hold values from 1 to 4096, as said below
- far_table: int32 [16, 256], P('grp'), may hold values from 0 to 527
- mig_src: int32 [128], P('grp'), may hold values from 0 to 7, as said below
- mig_page: int32 [128], P('grp'), may hold values from 0 to 511
Outputs:
- attn_out: bfloat16 [6144, 2048], P('grp', 'tp')
- accepted: bfloat16 [640, 8, 256], P('grp', 'tp')
The draws below stay inside these ranges and needn't reach their ends.
Inputs may be any that keep to these rules, and one draw needn't show every extreme that they name: `hidden`: entries within 4 times a scale of order one, with column scales spread over a factor of ten. `q_weight`: entries within 4 / sqrt(4608). `k_weight`: entries within 9 / sqrt(4608). `kv_pages`: finite, of order one, some key entries larger. `cache_len`: some request has exactly 4096 cached tokens. `tree_parent`: node 0 is the root with parent -1; nodes are ordered by depth and each parent is an earlier node one level up; depths are at most 4 and every tree has a node of depth 4. `pair_slot`: the 2 slots of a group differ. `far_len`: some entry is exactly 4096. `mig_src`: never the receiving group itself; at most 4 of a group's entries name one source, and in every group exactly 4 name one source.
All inputs are finite; a program needn't handle non-finite values.
Results may differ from the reference program's by a relative error of at most 0.012.
Values may be sent and summed in bfloat16 or wider, within the bound.
No kernel may reach another device: no remote copies, remote signals or barrier semaphores. Data moves between devices by JAX's collectives and lax.ppermute only.
A program may use at most 128 MiB of HBM per device.

```python
import jax
import jax.numpy as jnp
from jax import lax

D = 4608
QHEADS = 16
KVHEADS = 8
HEAD = 128
TREE = 48
PAGE = 16
MAXP = 256
LONG = 2
CAP = 4
ACCEPT = 5
REQ = 16
POOL = 512
MIGN = 16
SLOTS = 528
REQS = 128
TOKENS = 6144
N_GRP = 8


def draw_hidden(key, part):
    key = jax.random.fold_in(key, 11)
    column_key, row_key, value_key = jax.random.split(key, 3)
    column_scale = jnp.exp(jax.random.uniform(column_key, (D,), jnp.float32, -1.15, 1.15))
    row_scale = jnp.exp(jax.random.uniform(row_key, (TOKENS, 1), jnp.float32, -1.15, 1.15))
    values = jnp.clip(jax.random.normal(value_key, (TOKENS, D), jnp.float32), -4.0, 4.0)
    return (values * column_scale[None, :] * row_scale).astype(jnp.bfloat16)


def weight_pair(key):
    key = jax.random.fold_in(key, 23)
    query_key, noise_key = jax.random.split(key)
    query_part = jnp.clip(jax.random.normal(query_key, (D, QHEADS * HEAD), jnp.float32), -4.0, 4.0) * D ** (-0.5)
    paired = query_part.reshape(D, KVHEADS, 2, HEAD)
    noise = jnp.clip(jax.random.normal(noise_key, (D, KVHEADS, HEAD), jnp.float32), -4.0, 4.0) * D ** (-0.5)
    key_part = 0.6 * (paired[:, :, 0] + paired[:, :, 1]) + 0.5 * noise
    return (query_part, key_part.reshape(D, KVHEADS * HEAD))


def draw_q_weight(key, part):
    return weight_pair(key)[0].astype(jnp.bfloat16)


def draw_k_weight(key, part):
    return weight_pair(key)[1].astype(jnp.bfloat16)


def draw_kv_pages(key, part):
    key = jax.random.fold_in(key, 37)
    first_key, second_key = jax.random.split(key, 2)
    shape = (REQS // REQ * POOL, PAGE, KVHEADS, HEAD)
    key_half = 1.5 * jnp.clip(jax.random.normal(first_key, shape, jnp.float32), -5.0, 5.0)
    value_half = jnp.clip(jax.random.normal(second_key, shape, jnp.float32), -5.0, 5.0)
    return jnp.concatenate([key_half, value_half], -1).astype(jnp.bfloat16)


def draw_cache_len(key, part):
    key = jax.random.fold_in(key, 53)
    scale_key, length_key, where_key = jax.random.split(key, 3)
    groups = REQS // REQ
    ceiling_all = MAXP * PAGE
    factor = jax.random.randint(scale_key, (groups, 1), 1, 5)
    ceiling = jnp.maximum(ceiling_all * factor // 4, 1)
    lengths = jax.random.randint(length_key, (groups, REQ), 1, ceiling + 1).reshape(-1)
    target = jax.random.randint(where_key, (), 0, REQS)
    lengths = jnp.where(jnp.arange(REQS) == target, ceiling_all, lengths)
    return lengths.astype(jnp.int32)


def draw_far_len(key, part):
    key = jax.random.fold_in(key, 59)
    length_key, where_key = jax.random.split(key)
    groups = REQS // REQ
    ceiling_all = MAXP * PAGE
    lengths = jax.random.randint(length_key, (groups * LONG,), 1, ceiling_all + 1)
    target = jax.random.randint(where_key, (), 0, groups * LONG)
    lengths = jnp.where(jnp.arange(groups * LONG) == target, ceiling_all, lengths)
    return lengths.reshape(groups, LONG).astype(jnp.int32)


def draw_pair_slot(key, part):
    key = jax.random.fold_in(key, 61)
    groups = REQS // REQ

    def single(group_key):
        return jax.random.permutation(group_key, REQ)[:LONG]
    return jax.vmap(single)(jax.random.split(key, groups)).astype(jnp.int32)


def draw_tree_parent(key, part):
    key = jax.random.fold_in(key, 41)

    def single(tree_key):
        cut_key, pick_key = jax.random.split(tree_key)
        cuts = jnp.sort(jax.random.permutation(cut_key, TREE - 2)[:3] + 2).astype(jnp.int32)
        nodes = jnp.arange(TREE, dtype=jnp.int32)
        depths = (nodes >= 1).astype(jnp.int32) + (nodes >= cuts[0]).astype(jnp.int32) + (nodes >= cuts[1]).astype(jnp.int32) + (nodes >= cuts[2]).astype(jnp.int32)
        starts = jnp.concatenate([jnp.array([0, 1], jnp.int32), cuts, jnp.array([TREE], jnp.int32)])
        lower = starts[jnp.maximum(depths - 1, 0)]
        upper = jnp.maximum(starts[depths], lower + 1)
        picks = jax.random.randint(pick_key, (TREE,), lower, upper)
        return jnp.where(depths == 0, -1, picks).astype(jnp.int32)
    return jax.vmap(single)(jax.random.split(key, REQS))


def draw_mig_src(key, part):
    key = jax.random.fold_in(key, 71)
    groups = REQS // REQ

    def single(group, group_key):
        order_key, pick_key, shuffle_key = jax.random.split(group_key, 3)
        shuffled = jax.random.permutation(order_key, groups - 1).astype(jnp.int32)
        others = shuffled + (shuffled >= group).astype(jnp.int32)
        repeated = jnp.repeat(others[1:], CAP)
        picked = jax.random.permutation(pick_key, repeated)[:MIGN - CAP]
        entries = jnp.concatenate([jnp.full((CAP,), others[0], jnp.int32), picked])
        return jax.random.permutation(shuffle_key, entries)
    every = jax.vmap(single)(jnp.arange(groups, dtype=jnp.int32), jax.random.split(key, groups))
    return every.reshape(-1).astype(jnp.int32)


def set_ends(values, rng, smallest, top_value):
    longest = values.shape.index(max(values.shape))
    spots = []
    for shift in (0, 1):
        where = [jax.random.randint(jax.random.fold_in(rng, axis), (), 0, length) for axis, length in enumerate(values.shape)]
        where[longest] = (where[longest] + shift) % values.shape[longest]
        spots.append(tuple(where))
    return values.at[spots[0]].set(smallest).at[spots[1]].set(top_value)


def block_scale(own_key, dims, cuts, smallest, high):
    gain = 1.0
    for dim, parts in cuts:
        steps = jax.random.uniform(jax.random.fold_in(jax.random.fold_in(own_key, 6), dim), (parts,), jnp.float32, smallest / len(cuts), high / len(cuts))
        gain = gain * jnp.repeat(jnp.exp(steps), dims[dim] // parts).reshape((-1,) + (1,) * (len(dims) - 1 - dim))
    return gain


def centred(rng, shape, spread, most, cuts=(), held_as=jnp.bfloat16):
    values = spread * jax.random.normal(rng, shape, jnp.float32)
    if cuts:
        values = values * block_scale(rng, shape, cuts, -0.22, 0.18)
    return jnp.clip(values, -most, most).astype(held_as)


def setup_inputs(seed: int = 0) -> dict:
    seeds = jax.random.split(jax.random.key(seed), 16)
    hidden = draw_hidden(jax.random.fold_in(seeds[15], 71), 0)
    norm_gain = jnp.clip(1.0 + 0.18 * jax.random.normal(seeds[1], (D,), jnp.float32), 0.1, 1.9)
    q_weight = draw_q_weight(jax.random.fold_in(seeds[15], 71), 0)
    k_weight = draw_k_weight(jax.random.fold_in(seeds[15], 71), 0)
    v_weight = centred(seeds[4], (D, KVHEADS * HEAD), D ** -0.5, 0.09375, ((1, 4),))
    kv_pages = draw_kv_pages(jax.random.fold_in(seeds[15], 71), 0)
    page_table = set_ends(jax.random.randint(seeds[6], (REQS, MAXP), 0, SLOTS), jax.random.fold_in(seeds[6], 1), 0, SLOTS - 1).astype(jnp.int32)
    cache_len = draw_cache_len(jax.random.fold_in(seeds[15], 71), 0)
    tree_parent = draw_tree_parent(jax.random.fold_in(seeds[15], 71), 0)
    accept_node = set_ends(jax.random.randint(seeds[9], (REQS,), 0, TREE), jax.random.fold_in(seeds[9], 1), 0, TREE - 1).astype(jnp.int32)
    pair_slot = draw_pair_slot(jax.random.fold_in(seeds[15], 71), 0)
    far_len = draw_far_len(jax.random.fold_in(seeds[15], 71), 0)
    far_table = set_ends(jax.random.randint(seeds[12], (N_GRP * LONG, MAXP), 0, SLOTS), jax.random.fold_in(seeds[12], 1), 0, SLOTS - 1).astype(jnp.int32)
    mig_src = draw_mig_src(jax.random.fold_in(seeds[15], 71), 0)
    mig_page = set_ends(jax.random.randint(seeds[14], (N_GRP * MIGN,), 0, POOL), jax.random.fold_in(seeds[14], 1), 0, POOL - 1).astype(jnp.int32)
    return dict(hidden=hidden, norm_gain=norm_gain, q_weight=q_weight, k_weight=k_weight, v_weight=v_weight, kv_pages=kv_pages, page_table=page_table, cache_len=cache_len, tree_parent=tree_parent, accept_node=accept_node, pair_slot=pair_slot, far_len=far_len, far_table=far_table, mig_src=mig_src, mig_page=mig_page)


THETA_LOG = 9.210340371976184
SCORE_SCALE = 144.0 ** (-0.5)
LOGIT_CAP = 50.0
HIGHEST = lax.Precision.HIGHEST

def rotate(values, position):
    halfway = values.shape[-1] // 2
    angles = jnp.exp(-THETA_LOG * 2.0 * jnp.arange(halfway, dtype=jnp.float32) / values.shape[-1])
    phases = position.astype(jnp.float32)[:, None] * angles[None, :]
    cosine = jnp.cos(phases)[:, None, :]
    sine_part = jnp.sin(phases)[:, None, :]
    former = values[..., :halfway]
    latter = values[..., halfway:]
    return jnp.concatenate([former * cosine - latter * sine_part, latter * cosine + former * sine_part], -1)

def ancestry(parents):
    length = parents.shape[-1]
    labels = jnp.arange(length, dtype=jnp.int32)
    reached = (parents[..., :, None] == labels).astype(jnp.float32) + jnp.eye(length, dtype=jnp.float32)
    reached = jnp.minimum(jnp.einsum('nij,njk->nik', reached, reached, precision=HIGHEST), 1.0)
    reached = jnp.minimum(jnp.einsum('nij,njk->nik', reached, reached, precision=HIGHEST), 1.0)
    depths = lax.optimization_barrier(jnp.sum((reached > 0.5).astype(jnp.int32), -1)) - 1
    return (reached, depths)

def reference(hidden, norm_gain, q_weight, k_weight, v_weight, kv_pages, page_table, cache_len, tree_parent, accept_node, pair_slot, far_len, far_table, mig_src, mig_page):
    widened = hidden.astype(jnp.float32)
    row_scale = lax.rsqrt(lax.optimization_barrier(jnp.mean(widened * widened, axis=1)) + 1e-06)[:, None]
    scaled = (widened * norm_gain.astype(jnp.float32)[None, :]).astype(jnp.bfloat16)
    reached, depths = ancestry(tree_parent)
    slot_ids = jnp.arange(REQ, dtype=jnp.int32)
    matched = pair_slot[:, None, :] == slot_ids[None, :, None]
    far_own = lax.optimization_barrier(jnp.sum(jnp.where(matched, far_len[:, None, :], 0), -1)).reshape(-1)
    far_choice = lax.optimization_barrier(jnp.sum(jnp.where(matched, jnp.arange(LONG, dtype=jnp.int32)[None, None, :], 0), -1)).reshape(-1)
    long_flags = jnp.any(matched, -1).reshape(-1)
    position = ((cache_len + far_own)[:, None] + depths).reshape(-1)
    query_proj = jnp.dot(scaled, q_weight, preferred_element_type=jnp.float32) * row_scale
    queries = rotate(query_proj.reshape(TOKENS, QHEADS, HEAD), position).astype(jnp.bfloat16)
    key_proj = jnp.dot(scaled, k_weight, preferred_element_type=jnp.float32) * row_scale
    keys_new = rotate(key_proj.reshape(TOKENS, KVHEADS, HEAD), position).astype(jnp.bfloat16)
    value_proj = jnp.dot(scaled, v_weight, preferred_element_type=jnp.float32) * row_scale
    values_new = value_proj.astype(jnp.bfloat16).reshape(TOKENS, KVHEADS, HEAD)
    pools = kv_pages.reshape(N_GRP, POOL, PAGE, KVHEADS, 2 * HEAD)
    moved = pools[mig_src.reshape(N_GRP, MIGN), mig_page.reshape(N_GRP, MIGN)]
    extended = jnp.concatenate([pools, moved], 1)
    owners = jnp.arange(REQS, dtype=jnp.int32) // REQ
    offsets = jnp.arange(MAXP * PAGE, dtype=jnp.int32)

    def attend_one(packed):
        query_rows, key_rows, value_rows, table_row, own_length, tree_mask, owner, far_slot, long_flag = packed
        partner = owner + 1 - 2 * (owner % 2)
        own_cache = extended[owner, table_row].reshape(MAXP * PAGE, KVHEADS, 2 * HEAD)
        far_row = far_table[partner * LONG + far_slot]
        far_cache = extended[partner, far_row].reshape(MAXP * PAGE, KVHEADS, 2 * HEAD)
        far_length = far_len[owner, far_slot]
        all_keys = jnp.concatenate([own_cache[..., :HEAD], far_cache[..., :HEAD], key_rows], 0).astype(jnp.float32)
        all_values = jnp.concatenate([own_cache[..., HEAD:], far_cache[..., HEAD:], value_rows], 0).astype(jnp.float32)
        cache_ok = jnp.broadcast_to((offsets < own_length)[None, :], (TREE, MAXP * PAGE))
        far_ok = jnp.broadcast_to(((offsets < far_length) & long_flag)[None, :], (TREE, MAXP * PAGE))
        allowed = jnp.concatenate([cache_ok, far_ok, tree_mask > 0.5], 1)
        grouped = query_rows.reshape(TREE, KVHEADS, 2, HEAD).astype(jnp.float32)
        scores = jnp.einsum('igrd,tgd->igrt', grouped, all_keys, precision=HIGHEST) * SCORE_SCALE
        scores = LOGIT_CAP * jnp.tanh(scores / LOGIT_CAP)
        weights = jnp.where(allowed[:, None, None, :], jnp.exp(scores - LOGIT_CAP), 0.0)
        totals = lax.optimization_barrier(jnp.sum(weights, -1))
        rounded = weights.astype(jnp.bfloat16).astype(jnp.float32)
        mixed = jnp.einsum('igrt,tgd->igrd', rounded, all_values, precision=HIGHEST) / totals[..., None]
        return mixed.reshape(TREE, QHEADS * HEAD).astype(jnp.bfloat16)
    attn_out = lax.map(attend_one, (queries.reshape(REQS, TREE, QHEADS, HEAD), keys_new.reshape(REQS, TREE, KVHEADS, HEAD), values_new.reshape(REQS, TREE, KVHEADS, HEAD), page_table, cache_len, reached, owners, far_choice, long_flags)).reshape(TOKENS, QHEADS * HEAD)
    leaves = (jnp.arange(TREE, dtype=jnp.int32)[None, :] == accept_node[:, None]).astype(jnp.float32)
    lineage = jnp.einsum('rt,rtj->rj', leaves, reached, precision=HIGHEST)
    levels = (depths[:, None, :] == jnp.arange(ACCEPT, dtype=jnp.int32)[None, :, None]).astype(jnp.float32)
    picker = lineage[:, None, :] * levels
    fresh_rows = jnp.concatenate([keys_new, values_new], -1).reshape(REQS, TREE, KVHEADS * 2 * HEAD).astype(jnp.float32)
    accepted = jnp.einsum('rpt,rtc->rpc', picker, fresh_rows, precision=HIGHEST).astype(jnp.bfloat16).reshape(REQS * ACCEPT, KVHEADS, 2 * HEAD)
    return (attn_out, accepted)
```

```python
import jax
import jax.numpy as jnp
from jax import lax
from jax.experimental import pallas as pl
from jax.experimental.pallas import tpu as pltpu
from jax.sharding import PartitionSpec as P

D = 4608
CAP = 4
ACCEPT = 5


THETA_LOG = 9.210340371976184
SCORE_SCALE = 144.0 ** (-0.5)
LOGIT_CAP = 50.0
HIGHEST = lax.Precision.HIGHEST
IN_SCALE = SCORE_SCALE / LOGIT_CAP
OUT_SCALE = LOGIT_CAP * 1.4426950408889634
LANES = 128
BLOCK = 512
GROUPED = 2
MIB = 2**20
ANY = pl.BlockSpec(memory_space=pl.ANY)
VMEM = pl.BlockSpec(memory_space=pltpu.VMEM)
SMEM = pl.BlockSpec(memory_space=pltpu.SMEM)
BF16 = jnp.bfloat16
F32 = jnp.float32
I32 = jnp.int32


def estimate(micros):
    return pl.CostEstimate(flops=int(micros * 1.15e9), bytes_accessed=0, transcendentals=0)


def params(mib):
    return pltpu.CompilerParams(vmem_limit_bytes=mib * MIB)


def shape(dims, dtype):
    return jax.ShapeDtypeStruct(dims, dtype)


def aligned(index, unit):
    return pl.multiple_of(index * unit, unit)


def partner(value, axis, bit):
    mask = 2**bit
    pairs = [(source, source ^ mask) for source in range(lax.axis_size(axis))]
    return lax.ppermute(value, axis, pairs)


def rotate(values, position):
    halfway = values.shape[-1] // 2
    angles = jnp.exp(-THETA_LOG * 2.0 * jnp.arange(halfway, dtype=jnp.float32) / values.shape[-1])
    phases = position.astype(jnp.float32)[:, None] * angles[None, :]
    cosine = jnp.cos(phases)[:, None, :]
    sine_part = jnp.sin(phases)[:, None, :]
    former = values[..., :halfway]
    latter = values[..., halfway:]
    return jnp.concatenate(
        [former * cosine - latter * sine_part, latter * cosine + former * sine_part], -1
    )


def ancestry(parents):
    length = parents.shape[-1]
    labels = jnp.arange(length, dtype=jnp.int32)
    reached = (parents[..., :, None] == labels).astype(jnp.float32) + jnp.eye(
        length, dtype=jnp.float32
    )
    reached = jnp.minimum(jnp.einsum("nij,njk->nik", reached, reached, precision=HIGHEST), 1.0)
    reached = jnp.minimum(jnp.einsum("nij,njk->nik", reached, reached, precision=HIGHEST), 1.0)
    depths = jnp.sum((reached > 0.5).astype(jnp.int32), -1) - 1
    return (reached, depths)


def absorb(running, queries, keys_block, values_block, allowed):
    largest, summed, weighted = running
    scores = (
        jnp.einsum("igrd,tgd->igrt", queries, keys_block, preferred_element_type=jnp.float32)
        * SCORE_SCALE
    )
    scores = LOGIT_CAP * jnp.tanh(scores / LOGIT_CAP)
    weights = jnp.where(allowed, jnp.exp(scores - LOGIT_CAP), 0.0)
    summed = summed + jnp.sum(weights, -1)
    weighted = weighted + jnp.einsum(
        "igrt,tgd->igrd",
        weights.astype(jnp.bfloat16),
        values_block,
        preferred_element_type=jnp.float32,
    )
    return (largest, summed, weighted)


def empty_state(queries):
    leading = queries.shape[:3]
    return (
        jnp.full(leading, LOGIT_CAP, jnp.float32),
        jnp.zeros(leading, jnp.float32),
        jnp.zeros(queries.shape, jnp.float32),
    )


def attend_blocks(queries, loader, length, block_span):
    turns = (length + block_span - 1) // block_span

    def advance(number, running):
        keys_block, values_block = loader(number)
        allowed = (number * block_span + jnp.arange(block_span, dtype=jnp.int32) < length)[
            None, None, None, :
        ]
        return absorb(running, queries, keys_block, values_block, allowed)

    return lax.fori_loop(0, turns, advance, empty_state(queries))


def combine(states):
    summed = jnp.zeros(states[0][1].shape, jnp.float32)
    weighted = jnp.zeros(states[0][2].shape, jnp.float32)
    for state in states:
        summed = summed + state[1]
        weighted = weighted + state[2]
    return weighted / summed[..., None]


def general_body(
    hidden,
    norm_gain,
    q_weight,
    k_weight,
    v_weight,
    kv_pages,
    page_table,
    cache_len,
    tree_parent,
    accept_node,
    pair_slot,
    far_len,
    far_table,
    mig_src,
    mig_page,
):
    token_rows = hidden.shape[0]
    requests = cache_len.shape[0]
    tree_size = tree_parent.shape[1]
    head_size = kv_pages.shape[3] // 2
    local_heads = kv_pages.shape[2]
    page_size = kv_pages.shape[1]
    table_width = page_table.shape[1]
    long_count = pair_slot.shape[1]
    migrations = mig_src.shape[0]
    groups = lax.axis_size("grp")
    myself = lax.axis_index("grp")
    widened = lax.all_gather(hidden, "tp", axis=1, tiled=True).astype(jnp.float32)
    scaled = (widened * norm_gain[None, :]).astype(jnp.bfloat16)
    query_sum = jnp.dot(scaled, q_weight, preferred_element_type=jnp.float32)
    key_sum = jnp.dot(scaled, k_weight, preferred_element_type=jnp.float32)
    value_sum = jnp.dot(scaled, v_weight, preferred_element_type=jnp.float32)
    squares = jnp.sum(widened * widened, 1)
    query_sum, key_sum, value_sum, squares = (query_sum, key_sum, value_sum, squares)
    row_scale = lax.rsqrt(squares / D + 1e-06)[:, None]
    reached, depths = ancestry(tree_parent)
    far_mine = lax.dynamic_index_in_dim(far_len, myself, 0, keepdims=False)
    long_slots = pair_slot[0]
    matched = jnp.arange(requests, dtype=jnp.int32)[:, None] == long_slots[None, :]
    far_own = jnp.sum(jnp.where(matched, far_mine[None, :], 0), 1)
    position = ((cache_len + far_own)[:, None] + depths).reshape(-1)
    queries = rotate(
        (query_sum * row_scale).reshape(token_rows, 2 * local_heads, head_size), position
    ).astype(jnp.bfloat16)
    keys_new = rotate(
        (key_sum * row_scale).reshape(token_rows, local_heads, head_size), position
    ).astype(jnp.bfloat16)
    values_new = (
        (value_sum * row_scale).astype(jnp.bfloat16).reshape(token_rows, local_heads, head_size)
    )
    order_index = jnp.arange(migrations, dtype=jnp.int32)
    earlier = order_index[:, None] > order_index[None, :]

    def rank_of(sources):
        return jnp.sum(
            ((sources[..., :, None] == sources[..., None, :]) & earlier).astype(jnp.int32), -1
        )

    own_rank = rank_of(mig_src)
    slot_index = jnp.arange(CAP, dtype=jnp.int32)
    every_source, every_page = (
        lax.all_gather(mig_src, "grp", axis=0, tiled=True),
        lax.all_gather(mig_page, "grp", axis=0, tiled=True),
    )
    every_source = every_source.reshape(groups, migrations)
    every_page = every_page.reshape(groups, migrations)
    every_rank = rank_of(every_source)
    hits = (every_source[:, :, None] == myself) & (
        every_rank[:, :, None] == slot_index[None, None, :]
    )
    wanted = jnp.sum(jnp.where(hits, every_page[:, :, None] + 1, 0), 1) - 1
    present = (wanted >= 0)[:, :, None, None, None]
    outgoing = jnp.where(present, kv_pages[jnp.maximum(wanted, 0)], jnp.zeros((), jnp.bfloat16))
    incoming = lax.all_to_all(outgoing, "grp", split_axis=0, concat_axis=0, tiled=True)
    moved = incoming.reshape(groups * CAP, page_size, local_heads, 2 * head_size)[
        mig_src * CAP + own_rank
    ]
    extended = jnp.concatenate([kv_pages, moved], 0)
    block_pages = min(32, table_width)
    block_span = block_pages * page_size

    def page_loader(table_row):

        def loader(number):
            chosen = lax.dynamic_slice_in_dim(table_row, number * block_pages, block_pages, 0)
            gathered = extended[chosen].reshape(block_span, local_heads, 2 * head_size)
            return (gathered[..., :head_size], gathered[..., head_size:])

        return loader

    grouped = queries.reshape(requests, tree_size, local_heads, 2, head_size)
    long_queries = grouped[long_slots]
    far_dense = extended[far_table].reshape(
        long_count, table_width * page_size, local_heads, 2 * head_size
    )
    arrived = partner(far_dense, "grp", 0)

    def owner_part(packed):
        query_block, cache_block, length = packed

        def loader(number):
            portion = lax.dynamic_slice_in_dim(cache_block, number * block_span, block_span, 0)
            return (portion[..., :head_size], portion[..., head_size:])

        return attend_blocks(query_block, loader, length, block_span)

    far_parts = lax.map(owner_part, (long_queries, arrived, far_mine))
    keys_grouped = keys_new.reshape(requests, tree_size, local_heads, head_size)
    values_grouped = values_new.reshape(requests, tree_size, local_heads, head_size)

    def request_part(packed):
        query_block, key_block, value_block, table_row, length, tree_mask, match_row = packed
        own_state = attend_blocks(query_block, page_loader(table_row), length, block_span)
        tree_state = absorb(
            empty_state(query_block),
            query_block,
            key_block,
            value_block,
            (tree_mask > 0.5)[:, None, None, :],
        )
        chooser = match_row[:, None, None, None]
        far_state = (
            own_state[0],
            jnp.sum(jnp.where(chooser, far_parts[1], 0.0), 0),
            jnp.sum(jnp.where(match_row[:, None, None, None, None], far_parts[2], 0.0), 0),
        )
        mixed = combine((own_state, tree_state, far_state))
        return mixed.reshape(tree_size, 2 * local_heads * head_size).astype(jnp.bfloat16)

    attn_out = lax.map(
        request_part,
        (grouped, keys_grouped, values_grouped, page_table, cache_len, reached, matched),
    ).reshape(token_rows, 2 * local_heads * head_size)
    leaves = (jnp.arange(tree_size, dtype=jnp.int32)[None, :] == accept_node[:, None]).astype(
        jnp.float32
    )
    lineage = jnp.einsum("rt,rtj->rj", leaves, reached, precision=HIGHEST)
    levels = (depths[:, None, :] == jnp.arange(ACCEPT, dtype=jnp.int32)[None, :, None]).astype(
        jnp.float32
    )
    picker = lineage[:, None, :] * levels
    fresh_rows = (
        jnp.concatenate([keys_new, values_new], -1)
        .reshape(requests, tree_size, local_heads * 2 * head_size)
        .astype(jnp.float32)
    )
    accepted = (
        jnp.einsum("rpt,rtc->rpc", picker, fresh_rows, precision=HIGHEST)
        .astype(jnp.bfloat16)
        .reshape(requests * ACCEPT, local_heads, 2 * head_size)
    )
    return (attn_out, accepted)


def order_rows(hidden, pair_slot, cache_len, tree_size, counts):
    requests, longs = cache_len.shape[0], pair_slot.shape[1]
    first, later = counts[0], counts[1:]
    width = hidden.shape[1]

    def kernel(pair_ref, length_ref, hidden_ref, order_ref, rank_ref, *rest):
        outs, sem = rest[:-1], rest[-1]
        weight = []
        for i in range(requests):
            value = length_ref[i]
            for j in range(longs):
                value = value + jnp.where(pair_ref[0, j] == i, 1 << 20, 0)
            if i < first:
                value = value + ((first - i) << 24)
            weight.append(value)
        ranks = [jnp.int32(0)] * requests
        for i in range(requests):
            for j in range(i):
                ahead = (weight[j] >= weight[i]).astype(I32)
                ranks[i] = ranks[i] + ahead
                ranks[j] = ranks[j] + 1 - ahead
        for i in range(requests):
            order_ref[ranks[i]] = jnp.int32(i)
            rank_ref[i] = ranks[i]
        copies = []
        place = first
        for out, count in zip(outs, later, strict=True):
            for i in range(count):
                copies.append(
                    pltpu.make_async_copy(
                        hidden_ref.at[pl.ds(aligned(order_ref[place], tree_size), tree_size)],
                        out.at[pl.ds(i * tree_size, tree_size)],
                        sem.at[place],
                    )
                )
                copies[-1].start()
                place += 1
        for copy in copies:
            copy.wait()

    return pl.pallas_call(
        kernel,
        out_shape=[shape((requests,), I32)] * 2
        + [shape((count * tree_size, width), BF16) for count in later],
        in_specs=[SMEM, SMEM, ANY],
        out_specs=[SMEM, SMEM] + [ANY] * len(later),
        scratch_shapes=[pltpu.SemaphoreType.DMA((requests,))],
        cost_estimate=estimate(2),
        name="order_rows",
    )(pair_slot, cache_len, hidden)


def pick_pages(pool, wanted, page_size):
    peers, slots = wanted.shape
    width = pool.shape[1]

    def kernel(wanted_ref, pool_ref, *rest):
        outs, sem = rest[:-1], rest[-1]
        copies = []
        for peer in range(peers):
            for slot in range(slots):
                copies.append(
                    pltpu.make_async_copy(
                        pool_ref.at[pl.ds(aligned(wanted_ref[peer, slot], page_size), page_size)],
                        outs[peer].at[pl.ds(slot * page_size, page_size)],
                        sem.at[peer * slots + slot],
                    )
                )
                copies[-1].start()
        for copy in copies:
            copy.wait()

    return pl.pallas_call(
        kernel,
        out_shape=[shape((slots * page_size, width), BF16)] * peers,
        in_specs=[SMEM, ANY],
        out_specs=[ANY] * peers,
        scratch_shapes=[pltpu.SemaphoreType.DMA((peers * slots,))],
        cost_estimate=estimate(1.5),
        name="pick_pages",
    )(wanted, pool)


def project(
    places,
    static_rows,
    place_info,
    order,
    cache_len,
    pair_slot,
    far_mine,
    accept_node,
    parents,
    angles,
    gain,
    weights,
    hidden,
    hidden_core,
    from_x,
    from_xc,
    earlier,
):
    tree = parents.shape[0] // order.shape[0]
    count = len(places)
    rows = count * tree
    padded = -(-rows // LANES) * LANES
    quarter = hidden.shape[1]
    depth_all = gain.shape[0] * gain.shape[1]
    longs = pair_slot.shape[1]
    heads = weights[0].shape[1] // LANES
    kv_heads = weights[1].shape[1] // LANES
    share = heads // kv_heads
    per_item = heads * tree
    want_long = earlier is not None

    def kernel(*refs):
        (info_ref, order_ref, rank_ref, length_ref, pair_ref, far_ref, accept_ref) = refs[:7]
        (parents_ref, angles_ref, gain_ref, qw_ref, kw_ref, vw_ref) = refs[7:13]
        (own_ref, core_ref, x_ref, xc_ref) = refs[13:17]
        refs = refs[17:]
        if want_long:
            earlier_ref, refs = refs[0], refs[1:]
        q_out, acc_out, sum_out, picked_out = refs[:4]
        refs = refs[4:]
        if want_long:
            long_out, refs = refs[0], refs[1:]
        blocks, reached_ref, sem = refs
        requests = [order_ref[place] for place in places]
        copies = []
        for i, request in enumerate(requests):
            for part, source in enumerate((own_ref, core_ref)):
                copies.append(
                    pltpu.make_async_copy(
                        source.at[pl.ds(aligned(request, tree), tree)],
                        blocks.at[part, pl.ds(i * tree, tree)],
                        sem.at[len(copies)],
                    )
                )
        for part, source in ((2, x_ref), (3, xc_ref)):
            copies.append(pltpu.make_async_copy(source, blocks.at[part], sem.at[len(copies)]))
        for copy in copies:
            copy.start()
        filler = padded - rows
        column = [
            parents_ref[pl.ds(aligned(request, tree), tree), :] + 0 for request in requests
        ]
        column = [
            jnp.where(part < 0, -1, part + i * tree) for i, part in enumerate(column)
        ]
        if filler:
            column.append(jnp.full((filler, 1), -1, I32))
        column = jnp.concatenate(column, 0)
        labels = lax.broadcasted_iota(I32, (padded, padded), 1)
        mine = lax.broadcasted_iota(I32, (padded, padded), 0)
        step = ((column == labels) | (mine == labels)).astype(F32).astype(BF16)
        step = jnp.minimum(jnp.dot(step, step, preferred_element_type=F32), 1.0).astype(BF16)
        reached = jnp.minimum(jnp.dot(step, step, preferred_element_type=F32), 1.0)
        reached_ref[...] = reached
        reached_low = reached.astype(BF16)
        depth_column = jnp.sum(reached, 1, keepdims=True) - 1.0
        depth_row = (
            lax.dot_general(
                jnp.ones((16, padded), BF16),
                reached_low,
                (((1,), (1,)), ((), ())),
                preferred_element_type=F32,
            )
            - 1.0
        )
        bases = []
        for request in requests:
            base = length_ref[request]
            for j in range(longs):
                base = base + jnp.where(pair_ref[0, j] == request, far_ref[j], 0)
            bases.append(jnp.full((tree, 1), base, I32))
        position = jnp.concatenate(bases, 0).astype(F32) + depth_column[:rows]
        phases = position * angles_ref[...]
        cosine = jnp.cos(phases)
        half = LANES // 2
        sign = jnp.where(lax.broadcasted_iota(I32, (1, LANES), 1) < half, -1.0, 1.0)
        sine = jnp.sin(phases) * sign
        for copy in copies:
            copy.wait()
        sums = None
        squares = None
        me = info_ref[0]
        for part in range(4):
            which = me ^ part
            wide = blocks[part].astype(F32)
            square = jnp.sum(wide * wide, 1, keepdims=True)
            squares = square if squares is None else squares + square
            scaled = (wide * gain_ref[pl.ds(which, 1), :]).astype(BF16)
            terms = [
                jnp.dot(
                    scaled,
                    ref[pl.ds(aligned(which, quarter), quarter), :],
                    preferred_element_type=F32,
                )
                for ref in (qw_ref, kw_ref, vw_ref)
            ]
            sums = terms if sums is None else [a + b for a, b in zip(sums, terms, strict=True)]
        row_scale = lax.rsqrt(squares / depth_all + 1e-06)

        def rope(values):
            return (values * cosine + pltpu.roll(values, half, 1) * sine).astype(BF16)

        def head_of(values, h):
            return values[:, h * LANES : (h + 1) * LANES] * row_scale

        keys = [rope(head_of(sums[1], g)) for g in range(kv_heads)]
        values = [head_of(sums[2], g).astype(BF16) for g in range(kv_heads)]

        def pad(block):
            if not filler:
                return block
            return jnp.concatenate([block, jnp.zeros((filler, LANES), BF16)], 0)

        keys = [pad(block) for block in keys]
        values = [pad(block) for block in values]
        zeros = jnp.zeros((tree, LANES), BF16)
        for g in range(kv_heads):
            for r in range(share):
                query = rope(head_of(sums[0], g * share + r))
                scores = lax.dot_general(
                    query, keys[g], (((1,), (1,)), ((), ())), preferred_element_type=F32
                )
                exped = jnp.exp2(jnp.tanh(scores * IN_SCALE) * OUT_SCALE) * reached[:rows]
                total = exped[:, :LANES]
                for c in range(1, padded // LANES):
                    total = total + exped[:, c * LANES : (c + 1) * LANES]
                mixed = jnp.dot(exped.astype(BF16), values[g], preferred_element_type=F32)
                for i in range(count):
                    inside = slice(i * tree, (i + 1) * tree)
                    start = i * per_item + (g * share + r) * tree
                    there = slice(start, start + tree)
                    acc_out[there, :] = mixed[inside]
                    sum_out[there, :] = total[inside]
                    for other in range(kv_heads):
                        q_out[there, other * LANES : (other + 1) * LANES] = (
                            query[inside] if other == g else zeros
                        )
        levels = lax.broadcasted_iota(I32, (16, padded), 0).astype(F32)
        fresh = jnp.concatenate(
            [block for g in range(kv_heads) for block in (keys[g], values[g])], 1
        )
        picks = []
        for i, request in enumerate(requests):
            lineage = reached_ref[pl.ds(accept_ref[request] + i * tree, 1), :]
            picks.append(jnp.where(depth_row == levels, lineage, 0.0))
        picker = jnp.concatenate(picks, 0).astype(BF16)
        picked_out[...] = jnp.dot(picker, fresh, preferred_element_type=F32).astype(BF16)
        if want_long:
            before = earlier_ref.shape[0] // per_item
            for j in range(longs):
                place = rank_ref[pair_ref[0, j]]
                low = earlier_ref[pl.ds(aligned(jnp.minimum(place, before - 1), per_item), per_item), :]
                inside = jnp.clip(place - before, 0, count - 1)
                high = q_out[pl.ds(aligned(inside, per_item), per_item), :]
                long_out[j * per_item : (j + 1) * per_item, :] = jnp.where(
                    place < before, low, high
                )

    outs = [
        shape((count * per_item, kv_heads * LANES), BF16),
        shape((count * per_item, LANES), F32),
        shape((count * per_item, LANES), F32),
        shape((count * 16, kv_heads * 2 * LANES), BF16),
    ]
    operands = [
        place_info,
        order[:, 0],
        order[:, 1],
        cache_len,
        pair_slot,
        far_mine,
        accept_node,
        parents,
        angles,
        gain,
        *weights,
        hidden,
        hidden_core,
        from_x,
        from_xc,
    ]
    specs = [SMEM] * 7 + [VMEM] * 6 + [ANY] * 4
    if want_long:
        operands.append(earlier)
        specs.append(VMEM)
        outs.append(shape((longs * per_item, kv_heads * LANES), BF16))
    return pl.pallas_call(
        kernel,
        out_shape=outs,
        in_specs=specs,
        out_specs=[VMEM] * len(outs),
        scratch_shapes=[
            pltpu.VMEM((4, rows, quarter), BF16),
            pltpu.VMEM((padded, padded), F32),
            pltpu.SemaphoreType.DMA((2 * count + 2,)),
        ],
        compiler_params=params(56),
        cost_estimate=estimate(4),
        name=f"project_{places[0]}",
    )(*operands)


def attend(
    places,
    with_far,
    order,
    cache_len,
    pair_slot,
    far_len,
    table,
    queries,
    starts,
    totals,
    pool,
    moved,
    page_size,
    tree,
    out_buffer,
    token_rows,
    emit_long,
    merge,
):
    requests = cache_len.shape[0]
    longs = pair_slot.shape[1]
    per_item = starts[0].shape[0] // len(places) if len(starts) == 1 else None
    width = queries[0].shape[1]
    kv_heads = width // LANES
    pool_rows, pool_width = pool.shape
    own = len(places)
    count = own + (longs if with_far else 0)
    per_item = sum(q.shape[0] for q in queries) // count
    half = per_item // kv_heads
    heads = per_item // tree
    all_rows = pool_rows + sum(m.shape[0] for m in moved)
    table_width = table.shape[0] // (requests + longs)
    pages = BLOCK // page_size
    n_q, n_s, n_m = len(queries), len(starts), len(moved)
    n_copies = n_q + 2 * n_s + n_m + 4 + own

    def kernel(*refs):
        order_ref, rank_ref, length_ref, pair_ref, far_ref, table_ref = refs[:6]
        refs = refs[6:]
        q_refs, refs = refs[:n_q], refs[n_q:]
        start_refs, refs = refs[:n_s], refs[n_s:]
        total_refs, refs = refs[:n_s], refs[n_s:]
        pool_ref, refs = refs[0], refs[1:]
        moved_refs, refs = refs[:n_m], refs[n_m:]
        if merge is not None:
            (own_acc, own_sum, back_ref), refs = refs[:3], refs[3:]
        if out_buffer is not None:
            refs = refs[1:]
        out_ref, refs = refs[0], refs[1:]
        if emit_long:
            (long_acc, long_sum), refs = refs[:2], refs[2:]
        if with_far:
            far_out, refs = refs[0], refs[1:]
        (cache, qs, acc, sums, staged, lens, rows_of, sem) = refs[:8]
        score_refs = refs[8 : 8 + GROUPED]
        weight_refs = refs[8 + GROUPED :]
        copies = []

        def bring(source, target):
            copies.append(pltpu.make_async_copy(source, target, sem.at[len(copies)]))
            copies[-1].start()

        quarter = pool_rows // 4
        for c in range(4):
            span = pl.ds(c * quarter, quarter)
            bring(pool_ref.at[span], cache.at[span])
        at = pool_rows
        for ref in moved_refs:
            bring(ref, cache.at[pl.ds(at, ref.shape[0])])
            at += ref.shape[0]
        at = 0
        for ref in q_refs:
            bring(ref, qs.at[pl.ds(at, ref.shape[0])])
            at += ref.shape[0]
        at = 0
        for a, b in zip(start_refs, total_refs, strict=True):
            bring(a, acc.at[pl.ds(at, a.shape[0])])
            bring(b, sums.at[pl.ds(at, a.shape[0])])
            at += a.shape[0]
        if with_far:
            acc[own * per_item :, :] = jnp.zeros((longs * per_item, LANES), F32)
            sums[own * per_item :, :] = jnp.zeros((longs * per_item, LANES), F32)
        for i, place in enumerate(places):
            request = order_ref[place]
            lens[i] = length_ref[request]
            rows_of[i] = request * table_width
        if with_far:
            for j in range(longs):
                lens[own + j] = far_ref[j]
                rows_of[own + j] = (requests + j) * table_width
        blocks = jnp.int32(0)
        for i in range(count):
            blocks = blocks + (lens[i] + BLOCK - 1) // BLOCK
        for copy in copies:
            copy.wait()

        def following(state):
            item, block = state
            last = (block + 1) * BLOCK >= lens[item]
            return (
                jnp.where(last, jnp.minimum(item + 1, count - 1), item),
                jnp.where(last, 0, block + 1),
            )

        def gathered(state, first, size):
            item, block = state
            base = rows_of[item] + block * pages
            return jnp.concatenate(
                [
                    cache[
                        pl.ds(aligned(table_ref[base + j], page_size), page_size),
                        first : first + size,
                    ]
                    for j in range(pages)
                ],
                0,
            )

        def score(state, scores):
            item = state[0]
            scores[...] = lax.dot_general(
                qs[pl.ds(aligned(item, per_item), per_item), :],
                gathered(state, 0, width),
                (((1,), (1,)), ((), ())),
                preferred_element_type=F32,
            )

        def weigh(state, number, scores, weights):
            item, block = state
            left = jnp.where(number < blocks, lens[item] - block * BLOCK, 0)
            allowed = lax.broadcasted_iota(I32, (1, BLOCK), 1) < left
            exped = jnp.exp2(jnp.tanh(scores[...] * IN_SCALE) * OUT_SCALE)
            exped = jnp.where(allowed, exped, 0.0)
            weights[...] = exped.astype(BF16)
            part = exped[:, :LANES]
            for c in range(1, BLOCK // LANES):
                part = part + exped[:, c * LANES : (c + 1) * LANES]
            sums[pl.ds(aligned(item, per_item), per_item), :] += part

        def mix(state, weights):
            item = state[0]
            mixed = jnp.dot(
                weights[...], gathered(state, width, width), preferred_element_type=F32
            )
            for g in range(kv_heads):
                there = pl.ds(aligned(item * kv_heads + g, half), half)
                acc[there, :] += mixed[
                    g * half : (g + 1) * half, g * LANES : (g + 1) * LANES
                ]

        def group_from(state):
            states = [state]
            for _ in range(GROUPED - 1):
                states.append(following(states[-1]))
            return states, following(states[-1])

        group0, next0 = group_from((jnp.int32(0), jnp.int32(0)))
        for u in range(GROUPED):
            score(group0[u], score_refs[u])
        for u in range(GROUPED):
            weigh(group0[u], u, score_refs[u], weight_refs[u])
        group1, next1 = group_from(next0)
        for u in range(GROUPED):
            score(group1[u], score_refs[u])

        def turn(number, carried):
            state0, state1, state2 = carried
            now0, _ = group_from(state0)
            now1, _ = group_from(state1)
            now2, state3 = group_from(state2)
            for u in range(GROUPED):
                mix(now0[u], weight_refs[u])
                weigh(now1[u], (number + 1) * GROUPED + u, score_refs[u], weight_refs[u])
                score(now2[u], score_refs[u])
            return state1, state2, state3

        lax.fori_loop(
            0,
            (blocks + GROUPED - 1) // GROUPED,
            turn,
            ((jnp.int32(0), jnp.int32(0)), next0, next1),
        )

        def lay(target, block):
            for h in range(heads):
                target[:, h * LANES : (h + 1) * LANES] = block[h * tree : (h + 1) * tree].astype(
                    BF16
                )

        sent = []

        def put(number, request):
            sent.append(
                pltpu.make_async_copy(
                    staged.at[number],
                    out_ref.at[pl.ds(aligned(request, tree), tree)],
                    sem.at[number],
                )
            )
            sent[-1].start()

        for i, place in enumerate(places):
            there = slice(i * per_item, (i + 1) * per_item)
            total = jnp.sum(sums[there, :], 1, keepdims=True)
            lay(staged.at[i], acc[there, :] / total)
            put(i, order_ref[place])
        if merge is not None:
            for j in range(longs):
                there = slice(j * per_item, (j + 1) * per_item)
                total = jnp.sum(own_sum[there, :], 1, keepdims=True)
                total = total + back_ref[there, LANES : 2 * LANES].astype(F32)
                whole = own_acc[there, :] + back_ref[there, :LANES].astype(F32)
                lay(staged.at[own + j], whole / total)
                put(own + j, pair_ref[0, j])
        if emit_long:
            for j in range(longs):
                place = rank_ref[pair_ref[0, j]]
                there = slice(j * per_item, (j + 1) * per_item)
                here = pl.ds(aligned(jnp.minimum(place, own - 1), per_item), per_item)
                long_acc[there, :] = acc[here, :]
                long_sum[there, :] = sums[here, :]
        if with_far:
            far_rows = slice(own * per_item, count * per_item)
            total = jnp.sum(sums[far_rows, :], 1, keepdims=True)
            far_out[:, :LANES] = acc[far_rows, :].astype(BF16)
            far_out[:, LANES:] = jnp.broadcast_to(total, (longs * per_item, LANES)).astype(BF16)
        for copy in sent:
            copy.wait()

    operands = [
        order[:, 0],
        order[:, 1],
        cache_len,
        pair_slot,
        far_len,
        table,
        *queries,
        *starts,
        *totals,
        pool,
        *moved,
    ]
    specs = [SMEM] * 6 + [ANY] * (n_q + 2 * n_s + 1 + n_m)
    outs = [shape((token_rows, heads * LANES), BF16)]
    out_specs = [ANY]
    if merge is not None:
        operands += list(merge)
        specs += [VMEM] * 3
    aliases = {}
    if out_buffer is not None:
        aliases = {len(operands): 0}
        operands.append(out_buffer)
        specs.append(ANY)
    if emit_long:
        outs += [shape((longs * per_item, LANES), F32)] * 2
        out_specs += [VMEM] * 2
    if with_far:
        outs.append(shape((longs * per_item, 2 * LANES), BF16))
        out_specs.append(VMEM)
    return pl.pallas_call(
        kernel,
        out_shape=outs,
        in_specs=specs,
        out_specs=out_specs,
        scratch_shapes=[
            pltpu.VMEM((all_rows, pool_width), BF16),
            pltpu.VMEM((count * per_item, width), BF16),
            pltpu.VMEM((count * per_item, LANES), F32),
            pltpu.VMEM((count * per_item, LANES), F32),
            pltpu.VMEM((own + longs, tree, heads * LANES), BF16),
            pltpu.SMEM((count,), I32),
            pltpu.SMEM((count,), I32),
            pltpu.SemaphoreType.DMA((n_copies + longs,)),
            *[pltpu.VMEM((per_item, BLOCK), F32) for _ in range(GROUPED)],
            *[pltpu.VMEM((per_item, BLOCK), BF16) for _ in range(GROUPED)],
        ],
        input_output_aliases=aliases,
        compiler_params=params(56),
        cost_estimate=estimate(10 if with_far else 6),
        name=f"attend_{places[0]}",
    )(*operands)


def swap(value, axis, mask):
    pairs = [(source, source ^ mask) for source in range(lax.axis_size(axis))]
    return lax.ppermute(value, axis, pairs)


def body(
    hidden,
    norm_gain,
    q_weight,
    k_weight,
    v_weight,
    kv_pages,
    page_table,
    cache_len,
    tree_parent,
    accept_node,
    pair_slot,
    far_len,
    far_table,
    mig_src,
    mig_page,
):
    requests, tree = tree_parent.shape
    token_rows = hidden.shape[0]
    own_pages, page_size, kv_heads, entry = kv_pages.shape
    groups = lax.axis_size("grp")
    me = lax.axis_index("grp")
    spot = lax.axis_index("tp")
    counts = chunk_counts(requests)
    firsts = [sum(counts[:c]) for c in range(len(counts))]
    places = [list(range(f, f + n)) for f, n in zip(firsts, counts, strict=True)]

    order, rank, *rows = order_rows(hidden, pair_slot, cache_len, tree, counts)
    rows = [hidden[: counts[0] * tree], *rows]
    hidden_core = swap(hidden, "tp", 1)
    from_x = [swap(part, "tp", 2) for part in rows]
    from_xc = [swap(part, "tp", 1) for part in from_x]
    order = jnp.stack([order, rank], 1)

    migrations = mig_src.shape[0]
    index = jnp.arange(migrations, dtype=I32)
    earlier = (index[:, None] > index[None, :]) & (mig_src[:, None] == mig_src[None, :])
    slot = jnp.sum(earlier.astype(I32), 1)
    peers = jnp.arange(1, groups, dtype=I32)
    slots = jnp.arange(CAP, dtype=I32)
    peer_of = mig_src ^ me
    hits = (peer_of[None, None, :] == peers[:, None, None]) & (
        slot[None, None, :] == slots[None, :, None]
    )
    asked = jnp.sum(jnp.where(hits, mig_page[None, None, :], 0), -1)
    wanted = jnp.stack([swap(asked[k - 1], "grp", k) for k in range(1, groups)], 0)
    pool = (
        kv_pages.reshape(own_pages * page_size, kv_heads, 2, LANES)
        .transpose(0, 2, 1, 3)
        .reshape(own_pages * page_size, 2 * kv_heads * LANES)
    )
    outgoing = pick_pages(pool, wanted, page_size)
    moved = [swap(part, "grp", k + 1) for k, part in enumerate(outgoing)]
    placed = own_pages + (peer_of - 1) * CAP + slot
    tables = jnp.concatenate([page_table, far_table], 0)
    extra = tables[:, :, None] - own_pages == index[None, None, :]
    tables = jnp.where(
        tables < own_pages, tables, jnp.sum(jnp.where(extra, placed[None, None, :], 0), -1)
    ).reshape(-1)

    parents = tree_parent.reshape(-1, 1)
    half = LANES // 2
    angles = jnp.exp(-THETA_LOG * 2.0 * jnp.arange(half, dtype=F32) / LANES)
    angles = jnp.concatenate([angles, angles])[None, :]
    gain = norm_gain.reshape(-1, hidden.shape[1])
    info = jnp.full((1,), spot, I32)
    far_mine = lax.dynamic_index_in_dim(far_len, me, 0, keepdims=False)
    far_other = lax.dynamic_index_in_dim(far_len, me ^ 1, 0, keepdims=False)

    def chunk(c, before):
        return project(
            places[c],
            c == 0,
            info,
            order,
            cache_len,
            pair_slot,
            far_mine,
            accept_node,
            parents,
            angles,
            gain,
            (q_weight, k_weight, v_weight),
            hidden,
            hidden_core,
            from_x[c],
            from_xc[c],
            before,
        )

    parts = [chunk(0, None)]
    *second, long_queries = chunk(1, parts[0][0])
    parts.append(second)
    parts += [chunk(c, None) for c in range(2, len(counts))]
    far_queries = swap(long_queries, "grp", 1)

    def cached(cs, far, buffer, emit, merge):
        return attend(
            sum([places[c] for c in cs], []),
            far,
            order,
            cache_len,
            pair_slot,
            far_other,
            tables,
            [parts[c][0] for c in cs] + ([far_queries] if far else []),
            [parts[c][1] for c in cs],
            [parts[c][2] for c in cs],
            pool,
            moved,
            page_size,
            tree,
            buffer,
            token_rows,
            emit,
            merge,
        )

    out, long_acc, long_sum, far_done = cached([0, 1], True, None, True, None)
    back = swap(far_done, "grp", 1)
    (out,) = cached([2, 3], False, out, False, None)
    (out,) = cached([4], False, out, False, (long_acc, long_sum, back))
    picked = jnp.concatenate([part[3] for part in parts], 0).reshape(requests, 16, -1)
    accepted = (
        picked[rank, :ACCEPT].reshape(requests * ACCEPT, kv_heads, entry)
    )
    return (out, accepted)


def chunk_counts(requests):
    return (2, 4, 4, 4, requests - 14)


def solution(mesh):
    in_specs = (
        P("grp", "tp"),
        P(),
        P(None, "tp"),
        P(None, "tp"),
        P(None, "tp"),
        P("grp", None, "tp", None),
        P("grp", None),
        P("grp"),
        P("grp", None),
        P("grp"),
        P("grp", None),
        P(),
        P("grp", None),
        P("grp"),
        P("grp"),
    )
    out_specs = (P("grp", "tp"), P("grp", "tp", None))
    chosen = body if mesh.shape["tp"] == 4 else general_body
    return jax.shard_map(chosen, mesh=mesh, in_specs=in_specs, out_specs=out_specs, check_vma=False)
```

```python
import jax
import jax.numpy as jnp
from jax import lax
from jax.experimental import pallas as pl
from jax.experimental.pallas import tpu as pltpu
from jax.sharding import PartitionSpec as P

D = 4608
CAP = 4
ACCEPT = 5


THETA_LOG = 9.210340371976184
SCORE_SCALE = 144.0 ** (-0.5)
LOGIT_CAP = 50.0
HIGHEST = lax.Precision.HIGHEST
IN_SCALE = SCORE_SCALE / LOGIT_CAP
OUT_SCALE = LOGIT_CAP * 1.4426950408889634
LANES = 128
BLOCK = 256
GROUPED = 4
PAIR = 4
MIB = 2**20
ANY = pl.BlockSpec(memory_space=pl.ANY)
VMEM = pl.BlockSpec(memory_space=pltpu.VMEM)
SMEM = pl.BlockSpec(memory_space=pltpu.SMEM)
BF16 = jnp.bfloat16
F32 = jnp.float32
I32 = jnp.int32


def estimate(micros):
    return pl.CostEstimate(flops=int(micros * 1.15e9), bytes_accessed=0, transcendentals=0)


def params(mib):
    return pltpu.CompilerParams(vmem_limit_bytes=mib * MIB)


def shape(dims, dtype):
    return jax.ShapeDtypeStruct(dims, dtype)


def aligned(index, unit):
    return pl.multiple_of(index * unit, unit)


def partner(value, axis, bit):
    mask = 2**bit
    pairs = [(source, source ^ mask) for source in range(lax.axis_size(axis))]
    return lax.ppermute(value, axis, pairs)


def rotate(values, position):
    halfway = values.shape[-1] // 2
    angles = jnp.exp(-THETA_LOG * 2.0 * jnp.arange(halfway, dtype=jnp.float32) / values.shape[-1])
    phases = position.astype(jnp.float32)[:, None] * angles[None, :]
    cosine = jnp.cos(phases)[:, None, :]
    sine_part = jnp.sin(phases)[:, None, :]
    former = values[..., :halfway]
    latter = values[..., halfway:]
    return jnp.concatenate(
        [former * cosine - latter * sine_part, latter * cosine + former * sine_part], -1
    )


def ancestry(parents):
    length = parents.shape[-1]
    labels = jnp.arange(length, dtype=jnp.int32)
    reached = (parents[..., :, None] == labels).astype(jnp.float32) + jnp.eye(
        length, dtype=jnp.float32
    )
    reached = jnp.minimum(jnp.einsum("nij,njk->nik", reached, reached, precision=HIGHEST), 1.0)
    reached = jnp.minimum(jnp.einsum("nij,njk->nik", reached, reached, precision=HIGHEST), 1.0)
    depths = jnp.sum((reached > 0.5).astype(jnp.int32), -1) - 1
    return (reached, depths)


def absorb(running, queries, keys_block, values_block, allowed):
    largest, summed, weighted = running
    scores = (
        jnp.einsum("igrd,tgd->igrt", queries, keys_block, preferred_element_type=jnp.float32)
        * SCORE_SCALE
    )
    scores = LOGIT_CAP * jnp.tanh(scores / LOGIT_CAP)
    weights = jnp.where(allowed, jnp.exp(scores - LOGIT_CAP), 0.0)
    summed = summed + jnp.sum(weights, -1)
    weighted = weighted + jnp.einsum(
        "igrt,tgd->igrd",
        weights.astype(jnp.bfloat16),
        values_block,
        preferred_element_type=jnp.float32,
    )
    return (largest, summed, weighted)


def empty_state(queries):
    leading = queries.shape[:3]
    return (
        jnp.full(leading, LOGIT_CAP, jnp.float32),
        jnp.zeros(leading, jnp.float32),
        jnp.zeros(queries.shape, jnp.float32),
    )


def attend_blocks(queries, loader, length, block_span):
    turns = (length + block_span - 1) // block_span

    def advance(number, running):
        keys_block, values_block = loader(number)
        allowed = (number * block_span + jnp.arange(block_span, dtype=jnp.int32) < length)[
            None, None, None, :
        ]
        return absorb(running, queries, keys_block, values_block, allowed)

    return lax.fori_loop(0, turns, advance, empty_state(queries))


def combine(states):
    summed = jnp.zeros(states[0][1].shape, jnp.float32)
    weighted = jnp.zeros(states[0][2].shape, jnp.float32)
    for state in states:
        summed = summed + state[1]
        weighted = weighted + state[2]
    return weighted / summed[..., None]


def general_body(
    hidden,
    norm_gain,
    q_weight,
    k_weight,
    v_weight,
    kv_pages,
    page_table,
    cache_len,
    tree_parent,
    accept_node,
    pair_slot,
    far_len,
    far_table,
    mig_src,
    mig_page,
):
    token_rows = hidden.shape[0]
    requests = cache_len.shape[0]
    tree_size = tree_parent.shape[1]
    head_size = kv_pages.shape[3] // 2
    local_heads = kv_pages.shape[2]
    page_size = kv_pages.shape[1]
    table_width = page_table.shape[1]
    long_count = pair_slot.shape[1]
    migrations = mig_src.shape[0]
    groups = lax.axis_size("grp")
    myself = lax.axis_index("grp")
    widened = lax.all_gather(hidden, "tp", axis=1, tiled=True).astype(jnp.float32)
    scaled = (widened * norm_gain[None, :]).astype(jnp.bfloat16)
    query_sum = jnp.dot(scaled, q_weight, preferred_element_type=jnp.float32)
    key_sum = jnp.dot(scaled, k_weight, preferred_element_type=jnp.float32)
    value_sum = jnp.dot(scaled, v_weight, preferred_element_type=jnp.float32)
    squares = jnp.sum(widened * widened, 1)
    query_sum, key_sum, value_sum, squares = (query_sum, key_sum, value_sum, squares)
    row_scale = lax.rsqrt(squares / D + 1e-06)[:, None]
    reached, depths = ancestry(tree_parent)
    far_mine = lax.dynamic_index_in_dim(far_len, myself, 0, keepdims=False)
    long_slots = pair_slot[0]
    matched = jnp.arange(requests, dtype=jnp.int32)[:, None] == long_slots[None, :]
    far_own = jnp.sum(jnp.where(matched, far_mine[None, :], 0), 1)
    position = ((cache_len + far_own)[:, None] + depths).reshape(-1)
    queries = rotate(
        (query_sum * row_scale).reshape(token_rows, 2 * local_heads, head_size), position
    ).astype(jnp.bfloat16)
    keys_new = rotate(
        (key_sum * row_scale).reshape(token_rows, local_heads, head_size), position
    ).astype(jnp.bfloat16)
    values_new = (
        (value_sum * row_scale).astype(jnp.bfloat16).reshape(token_rows, local_heads, head_size)
    )
    order_index = jnp.arange(migrations, dtype=jnp.int32)
    earlier = order_index[:, None] > order_index[None, :]

    def rank_of(sources):
        return jnp.sum(
            ((sources[..., :, None] == sources[..., None, :]) & earlier).astype(jnp.int32), -1
        )

    own_rank = rank_of(mig_src)
    slot_index = jnp.arange(CAP, dtype=jnp.int32)
    every_source, every_page = (
        lax.all_gather(mig_src, "grp", axis=0, tiled=True),
        lax.all_gather(mig_page, "grp", axis=0, tiled=True),
    )
    every_source = every_source.reshape(groups, migrations)
    every_page = every_page.reshape(groups, migrations)
    every_rank = rank_of(every_source)
    hits = (every_source[:, :, None] == myself) & (
        every_rank[:, :, None] == slot_index[None, None, :]
    )
    wanted = jnp.sum(jnp.where(hits, every_page[:, :, None] + 1, 0), 1) - 1
    present = (wanted >= 0)[:, :, None, None, None]
    outgoing = jnp.where(present, kv_pages[jnp.maximum(wanted, 0)], jnp.zeros((), jnp.bfloat16))
    incoming = lax.all_to_all(outgoing, "grp", split_axis=0, concat_axis=0, tiled=True)
    moved = incoming.reshape(groups * CAP, page_size, local_heads, 2 * head_size)[
        mig_src * CAP + own_rank
    ]
    extended = jnp.concatenate([kv_pages, moved], 0)
    block_pages = min(32, table_width)
    block_span = block_pages * page_size

    def page_loader(table_row):

        def loader(number):
            chosen = lax.dynamic_slice_in_dim(table_row, number * block_pages, block_pages, 0)
            gathered = extended[chosen].reshape(block_span, local_heads, 2 * head_size)
            return (gathered[..., :head_size], gathered[..., head_size:])

        return loader

    grouped = queries.reshape(requests, tree_size, local_heads, 2, head_size)
    long_queries = grouped[long_slots]
    far_dense = extended[far_table].reshape(
        long_count, table_width * page_size, local_heads, 2 * head_size
    )
    arrived = partner(far_dense, "grp", 0)

    def owner_part(packed):
        query_block, cache_block, length = packed

        def loader(number):
            portion = lax.dynamic_slice_in_dim(cache_block, number * block_span, block_span, 0)
            return (portion[..., :head_size], portion[..., head_size:])

        return attend_blocks(query_block, loader, length, block_span)

    far_parts = lax.map(owner_part, (long_queries, arrived, far_mine))
    keys_grouped = keys_new.reshape(requests, tree_size, local_heads, head_size)
    values_grouped = values_new.reshape(requests, tree_size, local_heads, head_size)

    def request_part(packed):
        query_block, key_block, value_block, table_row, length, tree_mask, match_row = packed
        own_state = attend_blocks(query_block, page_loader(table_row), length, block_span)
        tree_state = absorb(
            empty_state(query_block),
            query_block,
            key_block,
            value_block,
            (tree_mask > 0.5)[:, None, None, :],
        )
        chooser = match_row[:, None, None, None]
        far_state = (
            own_state[0],
            jnp.sum(jnp.where(chooser, far_parts[1], 0.0), 0),
            jnp.sum(jnp.where(match_row[:, None, None, None, None], far_parts[2], 0.0), 0),
        )
        mixed = combine((own_state, tree_state, far_state))
        return mixed.reshape(tree_size, 2 * local_heads * head_size).astype(jnp.bfloat16)

    attn_out = lax.map(
        request_part,
        (grouped, keys_grouped, values_grouped, page_table, cache_len, reached, matched),
    ).reshape(token_rows, 2 * local_heads * head_size)
    leaves = (jnp.arange(tree_size, dtype=jnp.int32)[None, :] == accept_node[:, None]).astype(
        jnp.float32
    )
    lineage = jnp.einsum("rt,rtj->rj", leaves, reached, precision=HIGHEST)
    levels = (depths[:, None, :] == jnp.arange(ACCEPT, dtype=jnp.int32)[None, :, None]).astype(
        jnp.float32
    )
    picker = lineage[:, None, :] * levels
    fresh_rows = (
        jnp.concatenate([keys_new, values_new], -1)
        .reshape(requests, tree_size, local_heads * 2 * head_size)
        .astype(jnp.float32)
    )
    accepted = (
        jnp.einsum("rpt,rtc->rpc", picker, fresh_rows, precision=HIGHEST)
        .astype(jnp.bfloat16)
        .reshape(requests * ACCEPT, local_heads, 2 * head_size)
    )
    return (attn_out, accepted)


def order_rows(hidden, pair_slot, cache_len, mig_src, mig_page, own_pages, groups, tree_size, counts):
    requests, longs = cache_len.shape[0], pair_slot.shape[1]
    migrations = mig_src.shape[0]
    width = hidden.shape[1]

    def kernel(
        pair_ref, length_ref, source_ref, page_ref, hidden_ref, order_ref, rank_ref, asked, placed, *outs
    ):
        taken = [jnp.int32(0)] * migrations
        for i in range(migrations):
            for j in range(i):
                taken[i] = taken[i] + (source_ref[i] == source_ref[j]).astype(I32)
        for i in range(groups):
            for j in range(CAP):
                asked[i, j] = jnp.int32(0)
        for i in range(migrations):
            asked[source_ref[i], taken[i]] = page_ref[i]
            placed[i] = own_pages + source_ref[i] * CAP + taken[i]
        weight = []
        for i in range(requests):
            value = length_ref[i]
            for j in range(longs):
                value = value + jnp.where(pair_ref[0, j] == i, 1 << 20, 0)
            weight.append(value)
        ranks = [jnp.int32(0)] * requests
        for i in range(requests):
            for j in range(i):
                ahead = (weight[j] >= weight[i]).astype(I32)
                ranks[i] = ranks[i] + ahead
                ranks[j] = ranks[j] + 1 - ahead
        for i in range(requests):
            order_ref[ranks[i]] = jnp.int32(i)
            rank_ref[i] = ranks[i]
        place = 0
        for out, count in zip(outs, counts, strict=True):
            for i in range(count):
                out[pl.ds(i * tree_size, tree_size), :] = hidden_ref[
                    pl.ds(aligned(order_ref[place], tree_size), tree_size), :
                ]
                place += 1

    return pl.pallas_call(
        kernel,
        out_shape=[
            *[shape((requests,), I32)] * 2,
            shape((groups, CAP), I32),
            shape((migrations,), I32),
            *[shape((count * tree_size, width), BF16) for count in counts],
        ],
        in_specs=[SMEM] * 4 + [VMEM],
        out_specs=[SMEM] * 4 + [VMEM] * len(counts),
        cost_estimate=estimate(2),
        compiler_params=params(8),
        name="order_rows",
    )(*[hbm(a) for a in (pair_slot, cache_len, mig_src, mig_page)], hidden)


def pick_pages(pages, wanted):
    peers, slots = wanted.shape

    def kernel(wanted_ref, pages_ref, out, sem):
        copies = []
        for peer in range(peers):
            for slot in range(slots):
                copies.append(
                    pltpu.make_async_copy(
                        pages_ref.at[wanted_ref[peer, slot]],
                        out.at[peer, slot],
                        sem.at[peer * slots + slot],
                    )
                )
                copies[-1].start()
        for copy in copies:
            copy.wait()

    return pl.pallas_call(
        kernel,
        out_shape=shape((peers, slots, *pages.shape[1:]), BF16),
        in_specs=[SMEM, ANY],
        out_specs=VMEM,
        scratch_shapes=[pltpu.SemaphoreType.DMA((peers * slots,))],
        cost_estimate=estimate(1.5),
        compiler_params=params(4),
        name="pick_pages",
    )(wanted, hbm(pages))


def project_core(places, tree, longs, depth_all, info, inputs, scratch, q_ref, acc_ref, sum_ref, picked_out, long_out, started=lambda: None):
    (info_ref, order_ref, rank_ref, length_ref, pair_ref, far_ref, accept_ref) = info
    (parents_ref, angles_ref, gain_ref, *weight_refs, own_ref, core_ref, x_ref, xc_ref) = inputs
    (blocks, reached_ref, *kept, sem, weight_sem) = scratch
    count = len(places)
    paired = PAIR * tree
    padded = -(-paired // LANES) * LANES
    filler = padded - paired
    quarter = blocks.shape[2]
    heads = kept[0].shape[1] // LANES
    kv_heads = kept[1].shape[1] // LANES
    share = heads // kv_heads
    per_item = heads * tree
    requests = [order_ref[place] for place in places]
    me = info_ref[0]
    loads = []
    for part in range(4):
        span = pl.ds(aligned(me ^ part, quarter), quarter)
        loads.append([])
        for number, (source, target) in enumerate(zip(weight_refs, kept, strict=True)):
            loads[-1].append(
                pltpu.make_async_copy(
                    source.at[span], target.at[span], weight_sem.at[part, number]
                )
            )
    arrivals = [[], [], [], []]
    number = 0
    for part, source in enumerate((own_ref, core_ref)):
        for i, request in enumerate(requests):
            arrivals[part].append(
                pltpu.make_async_copy(
                    source.at[pl.ds(aligned(request, tree), tree)],
                    blocks.at[part, pl.ds(i * tree, tree)],
                    sem.at[number],
                )
            )
            number += 1
    for part, source in ((2, x_ref), (3, xc_ref)):
        arrivals[part].append(pltpu.make_async_copy(source, blocks.at[part], sem.at[number]))
        number += 1
    for part in range(4):
        for copy in arrivals[part] + loads[part]:
            copy.start()
    started()
    labels = lax.broadcasted_iota(I32, (padded, padded), 1)
    mine = lax.broadcasted_iota(I32, (padded, padded), 0)
    reached, depth_columns, depth_rows = [], [], []
    for p in range(count // PAIR):
        column = []
        for i in range(PAIR):
            part = parents_ref[pl.ds(aligned(requests[p * PAIR + i], tree), tree), :]
            column.append(jnp.where(part < 0, -1, part + i * tree))
        column = jnp.concatenate([*column, jnp.full((filler, 1), -1, I32)], 0)
        step = ((column == labels) | (mine == labels)).astype(F32).astype(BF16)
        step = jnp.minimum(jnp.dot(step, step, preferred_element_type=F32), 1.0).astype(BF16)
        whole = jnp.minimum(jnp.dot(step, step, preferred_element_type=F32), 1.0)
        reached_ref[p * padded : (p + 1) * padded, :] = whole
        reached.append(whole[:paired])
        depth_columns.append(jnp.sum(whole[:paired], 1, keepdims=True) - 1.0)
        depth_rows.append(
            lax.dot_general(
                jnp.ones((16, padded), BF16),
                whole.astype(BF16),
                (((1,), (1,)), ((), ())),
                preferred_element_type=F32,
            )
            - 1.0
        )
    bases = []
    for request in requests:
        base = length_ref[request]
        for j in range(longs):
            base = base + jnp.where(pair_ref[0, j] == request, far_ref[j], 0)
        bases.append(jnp.full((tree, 1), base, I32))
    position = jnp.concatenate(bases, 0).astype(F32) + jnp.concatenate(depth_columns, 0)
    phases = position * angles_ref[...]
    cosine = jnp.cos(phases)
    half = LANES // 2
    sign = jnp.where(lax.broadcasted_iota(I32, (1, LANES), 1) < half, -1.0, 1.0)
    sine = jnp.sin(phases) * sign
    sums = None
    squares = None
    for part in range(4):
        which = me ^ part
        for copy in arrivals[part] + loads[part]:
            copy.wait()
        wide = blocks[part].astype(F32)
        square = jnp.sum(wide * wide, 1, keepdims=True)
        squares = square if squares is None else squares + square
        scaled = (wide * gain_ref[pl.ds(which, 1), :]).astype(BF16)
        terms = [
            jnp.dot(
                scaled,
                ref[pl.ds(aligned(which, quarter), quarter), :],
                preferred_element_type=F32,
            )
            for ref in kept
        ]
        sums = terms if sums is None else [a + b for a, b in zip(sums, terms, strict=True)]
    row_scale = lax.rsqrt(squares / depth_all + 1e-06)

    def rope(values):
        return (values * cosine + pltpu.roll(values, half, 1) * sine).astype(BF16)

    def head_of(values, h):
        return values[:, h * LANES : (h + 1) * LANES] * row_scale

    keys = [rope(head_of(sums[1], g)) for g in range(kv_heads)]
    values = [head_of(sums[2], g).astype(BF16) for g in range(kv_heads)]

    def pad(block):
        return jnp.concatenate([block, jnp.zeros((filler, LANES), BF16)], 0)

    queries = [rope(head_of(sums[0], h)) for h in range(heads)]
    zeros = jnp.zeros((tree, LANES), BF16)
    levels = lax.broadcasted_iota(I32, (16, padded), 0).astype(F32)
    pairs = range(count // PAIR)
    cuts = [slice(p * paired, (p + 1) * paired) for p in pairs]
    pair_keys = [[pad(block[cut]) for block in keys] for cut in cuts]
    pair_values = [[pad(block[cut]) for block in values] for cut in cuts]
    each = [(p, g) for p in pairs for g in range(kv_heads)]
    scores = [
        lax.dot_general(
            jnp.concatenate([queries[g * share + r][cuts[p]] for r in range(share)], 0),
            pair_keys[p][g],
            (((1,), (1,)), ((), ())),
            preferred_element_type=F32,
        )
        for p, g in each
    ]
    masks = [jnp.concatenate([block] * share, 0) for block in reached]
    exped = [
        jnp.exp2(jnp.tanh(score * IN_SCALE) * OUT_SCALE) * masks[p]
        for (p, g), score in zip(each, scores, strict=True)
    ]
    mixed = [
        jnp.dot(block.astype(BF16), pair_values[p][g], preferred_element_type=F32)
        for (p, g), block in zip(each, exped, strict=True)
    ]
    pickers = []
    for p in pairs:
        picks = []
        for i in range(PAIR):
            leaf = accept_ref[requests[p * PAIR + i]] + p * padded + i * tree
            picks.append(jnp.where(depth_rows[p] == levels, reached_ref[pl.ds(leaf, 1), :], 0.0))
        pickers.append(jnp.concatenate(picks, 0).astype(BF16))
    picked = []
    for p in pairs:
        fresh = [block for g in range(kv_heads) for block in (pair_keys[p][g], pair_values[p][g])]
        picked.append(
            jnp.dot(pickers[p], jnp.concatenate(fresh, 1), preferred_element_type=F32)
        )
    for (p, g), block, weight in zip(each, mixed, exped, strict=True):
        total = weight[:, :LANES]
        for c in range(1, padded // LANES):
            total = total + weight[:, c * LANES : (c + 1) * LANES]
        for r in range(share):
            h = g * share + r
            for i in range(PAIR):
                start = (p * PAIR + i) * per_item + h * tree
                there = slice(start, start + tree)
                inside = slice(r * paired + i * tree, r * paired + (i + 1) * tree)
                acc_ref[there, :] = block[inside]
                sum_ref[there, :] = total[inside]
                first = p * paired + i * tree
                for other in range(kv_heads):
                    q_ref[there, other * LANES : (other + 1) * LANES] = (
                        queries[h][first : first + tree] if other == g else zeros
                    )
    for p in pairs:
        picked_out[p * PAIR * 16 : (p + 1) * PAIR * 16, :] = picked[p].astype(BF16)
    if long_out is not None:
        for j in range(longs):
            place = rank_ref[pair_ref[0, j]]
            long_out[j * per_item : (j + 1) * per_item, :] = q_ref[
                pl.ds(aligned(place, per_item), per_item), :
            ]


def project_scratch(count, tree, hidden, weights):
    padded = -(-PAIR * tree // LANES) * LANES
    return [
        pltpu.VMEM((4, count * tree, hidden.shape[1]), BF16),
        pltpu.VMEM((count // PAIR * padded, padded), F32),
        *[pltpu.VMEM(weight.shape, BF16) for weight in weights],
        pltpu.SemaphoreType.DMA((2 * count + 2,)),
        pltpu.SemaphoreType.DMA((4, len(weights))),
    ]


def state_scratch(count, per_item, width):
    return [
        pltpu.VMEM((count * per_item, width), BF16),
        pltpu.VMEM((count * per_item, LANES), F32),
        pltpu.VMEM((count * per_item, LANES), F32),
    ]


def hbm(array):
    return pltpu.with_memory_space_constraint(array, pltpu.HBM)


def project_first(places, tree, longs, scalars, tables, weights, parts):
    count = len(places)
    hidden = parts[0]
    heads = weights[0].shape[1] // LANES
    width = weights[1].shape[1]
    per_item = heads * tree
    depth_all = weights[0].shape[0]
    n_scratch = len(project_scratch(count, tree, hidden, weights))

    def kernel(*refs):
        info, refs = refs[:7], refs[7:]
        inputs, refs = refs[:10], refs[10:]
        outs, (picked_out, long_out), refs = refs[:3], refs[3:5], refs[5:]
        state, scratch, sem = refs[:3], refs[3 : 3 + n_scratch], refs[-1]
        project_core(
            places, tree, longs, depth_all, info, inputs, scratch, *state, picked_out, long_out
        )
        copies = [
            pltpu.make_async_copy(source, target, sem.at[i])
            for i, (source, target) in enumerate(zip(state, outs, strict=True))
        ]
        for copy in copies:
            copy.start()
        for copy in copies:
            copy.wait()

    rows = count * per_item
    return pl.pallas_call(
        kernel,
        out_shape=[
            pltpu.HBM((rows, width), BF16),
            pltpu.HBM((rows, LANES), F32),
            pltpu.HBM((rows, LANES), F32),
            shape((count * 16, 2 * width), BF16),
            shape((longs * per_item, width), BF16),
        ],
        in_specs=[SMEM] * 7 + [VMEM] * 3 + [ANY] * 7,
        out_specs=[ANY] * 3 + [VMEM] * 2,
        scratch_shapes=[
            *state_scratch(count, per_item, width),
            *project_scratch(count, tree, hidden, weights),
            pltpu.SemaphoreType.DMA((3,)),
        ],
        compiler_params=params(40),
        cost_estimate=estimate(1),
        name="project_first",
    )(*scalars, *tables, *[hbm(a) for a in (*weights, *parts)])


def attend_core(lens, rows_of, table_ref, cache, qs, acc, sums, score_refs, weight_refs, page_size):
    count = lens.shape[0]
    width = qs.shape[1]
    kv_heads = width // LANES
    per_item = qs.shape[0] // count
    half = per_item // kv_heads
    pages = BLOCK // page_size
    blocks = jnp.int32(0)
    for i in range(count):
        blocks = blocks + (lens[i] + BLOCK - 1) // BLOCK
    def following(state):
        item, block = state
        last = (block + 1) * BLOCK >= lens[item]
        return (
            jnp.where(last, jnp.minimum(item + 1, count - 1), item),
            jnp.where(last, 0, block + 1),
        )

    def gathered(state, first):
        item, block = state
        base = rows_of[item] + block * pages
        spans = [
            pl.ds(aligned(table_ref[base + j], page_size), page_size) for j in range(pages)
        ]
        sides = []
        for g in range(kv_heads):
            lanes = slice((2 * g + first) * LANES, (2 * g + first + 1) * LANES)
            sides.append(jnp.concatenate([cache[span, lanes] for span in spans], 0))
        return jnp.concatenate(sides, 1)

    def score(state, scores):
        item = state[0]
        scores[...] = lax.dot_general(
            qs[pl.ds(aligned(item, per_item), per_item), :],
            gathered(state, 0),
            (((1,), (1,)), ((), ())),
            preferred_element_type=F32,
        )

    def weigh(state, number, scores, weights):
        item, block = state
        left = jnp.where(number < blocks, lens[item] - block * BLOCK, 0)
        allowed = lax.broadcasted_iota(I32, (1, BLOCK), 1) < left
        exped = jnp.exp2(jnp.tanh(scores[...] * IN_SCALE) * OUT_SCALE)
        exped = jnp.where(allowed, exped, 0.0)
        weights[...] = exped.astype(BF16)
        part = exped[:, :LANES]
        for c in range(1, BLOCK // LANES):
            part = part + exped[:, c * LANES : (c + 1) * LANES]
        sums[pl.ds(aligned(item, per_item), per_item), :] += part

    def mix(state, weights):
        item = state[0]
        mixed = jnp.dot(
            weights[...], gathered(state, 1), preferred_element_type=F32
        )
        for g in range(kv_heads):
            there = pl.ds(aligned(item * kv_heads + g, half), half)
            acc[there, :] += mixed[
                g * half : (g + 1) * half, g * LANES : (g + 1) * LANES
            ]

    def group_from(state):
        states = [state]
        for _ in range(GROUPED - 1):
            states.append(following(states[-1]))
        return states, following(states[-1])

    group0, next0 = group_from((jnp.int32(0), jnp.int32(0)))
    for u in range(GROUPED):
        score(group0[u], score_refs[u])
    for u in range(GROUPED):
        weigh(group0[u], u, score_refs[u], weight_refs[u])
    group1, next1 = group_from(next0)
    for u in range(GROUPED):
        score(group1[u], score_refs[u])

    def turn(number, carried):
        state0, state1, state2 = carried
        now0, _ = group_from(state0)
        now1, _ = group_from(state1)
        now2, state3 = group_from(state2)
        for u in range(GROUPED):
            mix(now0[u], weight_refs[u])
            weigh(now1[u], (number + 1) * GROUPED + u, score_refs[u], weight_refs[u])
            score(now2[u], score_refs[u])
        return state1, state2, state3

    lax.fori_loop(
        0,
        (blocks + GROUPED - 1) // GROUPED,
        turn,
        ((jnp.int32(0), jnp.int32(0)), next0, next1),
    )


def attend_scratch(count, per_item, cache_rows, cache_width):
    return [
        pltpu.VMEM((cache_rows, cache_width), BF16),
        pltpu.SMEM((count,), I32),
        pltpu.SMEM((count,), I32),
        *[pltpu.VMEM((per_item, BLOCK), F32) for _ in range(GROUPED)],
        *[pltpu.VMEM((per_item, BLOCK), BF16) for _ in range(GROUPED)],
    ]


def lay(target, block, tree):
    for h in range(block.shape[0] // tree):
        target[:, h * LANES : (h + 1) * LANES] = block[h * tree : (h + 1) * tree].astype(
            BF16
        )


def bring_cache(pool_ref, moved_ref, cache, sem):
    rows = pool_ref.shape[0]
    quarter = rows // 4
    copies = [
        pltpu.make_async_copy(
            pool_ref.at[pl.ds(c * quarter, quarter)],
            cache.at[pl.ds(c * quarter, quarter)],
            sem.at[c],
        )
        for c in range(4)
    ]
    copies.append(
        pltpu.make_async_copy(moved_ref, cache.at[pl.ds(rows, moved_ref.shape[0])], sem.at[4])
    )
    for copy in copies:
        copy.start()
    return copies


def send_out(number, request, staged, out_ref, sem, tree):
    copy = pltpu.make_async_copy(
        staged.at[number], out_ref.at[pl.ds(aligned(request, tree), tree)], sem.at[number]
    )
    copy.start()
    return copy


def attend_first(
    places, tree, longs, requests, scalars, far_len, table, state, far_queries, pool, moved, page_size, token_rows
):
    own = len(places)
    count = own + longs
    rows, width = state[0].shape
    per_item = rows // own
    heads = per_item // tree
    far_rows = longs * per_item
    table_width = table.shape[0] // (requests + longs)
    cache_rows, cache_width = pool.shape[0] + moved.shape[0], pool.shape[1]

    def kernel(*refs):
        (order_ref, rank_ref, length_ref, pair_ref, far_ref, table_ref), refs = refs[:6], refs[6:]
        state_refs, (far_q, pool_ref, moved_ref), refs = refs[:3], refs[3:6], refs[6:]
        (out_ref, long_acc, long_sum, far_out), refs = refs[:4], refs[4:]
        (qs, acc, sums), (staged, sem, cache_sem), refs = refs[:3], refs[3:6], refs[6:]
        (cache, lens, rows_of), refs = refs[:3], refs[3:]
        copies = bring_cache(pool_ref, moved_ref, cache, cache_sem)
        for i, (source, target) in enumerate(zip(state_refs, (qs, acc, sums), strict=True)):
            copies.append(pltpu.make_async_copy(source, target.at[pl.ds(0, rows)], sem.at[i]))
            copies[-1].start()
        copies.append(pltpu.make_async_copy(far_q, qs.at[pl.ds(rows, far_rows)], sem.at[3]))
        copies[-1].start()
        acc[rows:, :] = jnp.zeros((far_rows, LANES), F32)
        sums[rows:, :] = jnp.zeros((far_rows, LANES), F32)
        for i, place in enumerate(places):
            request = order_ref[place]
            lens[i] = length_ref[request]
            rows_of[i] = request * table_width
        for j in range(longs):
            lens[own + j] = far_ref[j]
            rows_of[own + j] = (requests + j) * table_width
        for copy in copies:
            copy.wait()
        attend_core(
            lens, rows_of, table_ref, cache, qs, acc, sums, refs[:GROUPED], refs[GROUPED:], page_size
        )
        total = jnp.sum(sums[rows:, :], 1, keepdims=True)
        far_out[:, :LANES] = acc[rows:, :].astype(BF16)
        far_out[:, LANES:] = jnp.broadcast_to(total, (far_rows, LANES)).astype(BF16)
        sent = []
        for i, place in enumerate(places):
            there = slice(i * per_item, (i + 1) * per_item)
            lay(staged.at[i], acc[there, :] / jnp.sum(sums[there, :], 1, keepdims=True), tree)
            sent.append(send_out(i, order_ref[place], staged, out_ref, sem, tree))
        for j in range(longs):
            there = slice(j * per_item, (j + 1) * per_item)
            here = pl.ds(aligned(rank_ref[pair_ref[0, j]], per_item), per_item)
            long_acc[there, :] = acc[here, :]
            long_sum[there, :] = sums[here, :]
        for copy in sent:
            copy.wait()

    return pl.pallas_call(
        kernel,
        out_shape=[
            pltpu.HBM((token_rows, heads * LANES), BF16),
            shape((far_rows, LANES), F32),
            shape((far_rows, LANES), F32),
            shape((far_rows, 2 * LANES), BF16),
        ],
        in_specs=[SMEM] * 6 + [ANY] * 6,
        out_specs=[ANY] + [VMEM] * 3,
        scratch_shapes=[
            *state_scratch(count, per_item, width),
            pltpu.VMEM((own, tree, heads * LANES), BF16),
            pltpu.SemaphoreType.DMA((max(own, 4),)),
            pltpu.SemaphoreType.DMA((5,)),
            *attend_scratch(count, per_item, cache_rows, cache_width),
        ],
        compiler_params=params(32),
        cost_estimate=estimate(18),
        name="attend_first",
    )(*scalars, far_len, table, *[hbm(a) for a in (*state, far_queries, pool, moved)])


def finish(
    places, tree, longs, requests, scalars, tables, weights, parts, table, pool, moved, page_size, out
):
    own = len(places)
    hidden = parts[0]
    heads = weights[0].shape[1] // LANES
    width = weights[1].shape[1]
    per_item = heads * tree
    depth_all = weights[0].shape[0]
    n_scratch = len(project_scratch(own, tree, hidden, weights))
    table_width = table.shape[0] // (requests + longs)
    cache_rows, cache_width = pool.shape[0] + moved.shape[0], pool.shape[1]

    def kernel(*refs):
        info, table_ref, refs = refs[:7], refs[7], refs[8:]
        order_ref, length_ref = info[1], info[3]
        inputs, refs = refs[:10], refs[10:]
        (pool_ref, moved_ref), refs = refs[:2], refs[3:]
        (out_ref, picked_out), refs = refs[:2], refs[2:]
        (qs, acc, sums), (staged, sem, cache_sem), refs = refs[:3], refs[3:6], refs[6:]
        scratch, refs = refs[:n_scratch], refs[n_scratch:]
        (cache, lens, rows_of), refs = refs[:3], refs[3:]
        for i, place in enumerate(places):
            request = order_ref[place]
            lens[i] = length_ref[request]
            rows_of[i] = request * table_width
        copies = []
        project_core(
            places, tree, longs, depth_all, info, inputs, scratch, qs, acc, sums, picked_out, None,
            lambda: copies.extend(bring_cache(pool_ref, moved_ref, cache, cache_sem)),
        )
        for copy in copies:
            copy.wait()
        attend_core(
            lens, rows_of, table_ref, cache, qs, acc, sums, refs[:GROUPED], refs[GROUPED:], page_size
        )
        sent = []
        for i, place in enumerate(places):
            there = slice(i * per_item, (i + 1) * per_item)
            lay(staged.at[i], acc[there, :] / jnp.sum(sums[there, :], 1, keepdims=True), tree)
            sent.append(send_out(i, order_ref[place], staged, out_ref, sem, tree))
        for copy in sent:
            copy.wait()

    operands = [*scalars, table, *tables]
    operands += [hbm(a) for a in (*weights, *parts, pool, moved, out)]
    return pl.pallas_call(
        kernel,
        out_shape=[pltpu.HBM(out.shape, BF16), shape((own * 16, 2 * width), BF16)],
        in_specs=[SMEM] * 8 + [VMEM] * 3 + [ANY] * 10,
        out_specs=[ANY, VMEM],
        scratch_shapes=[
            *state_scratch(own, per_item, width),
            pltpu.VMEM((own, tree, heads * LANES), BF16),
            pltpu.SemaphoreType.DMA((own,)),
            pltpu.SemaphoreType.DMA((5,)),
            *project_scratch(own, tree, hidden, weights),
            *attend_scratch(own, per_item, cache_rows, cache_width),
        ],
        input_output_aliases={len(operands) - 1: 0},
        compiler_params=params(48),
        cost_estimate=estimate(18),
        name="finish",
    )(*operands)


def merge(tree, pair_slot, own_acc, own_sum, back, out):
    longs = pair_slot.shape[1]
    per_item = own_acc.shape[0] // longs
    heads = per_item // tree

    def kernel(pair_ref, acc_ref, sum_ref, back_ref, _, out_ref, staged, sem):
        sent = []
        for j in range(longs):
            there = slice(j * per_item, (j + 1) * per_item)
            total = jnp.sum(sum_ref[there, :], 1, keepdims=True)
            total = total + back_ref[there, LANES : 2 * LANES].astype(F32)
            whole = acc_ref[there, :] + back_ref[there, :LANES].astype(F32)
            lay(staged.at[j], whole / total, tree)
            sent.append(send_out(j, pair_ref[0, j], staged, out_ref, sem, tree))
        for copy in sent:
            copy.wait()

    return pl.pallas_call(
        kernel,
        out_shape=pltpu.HBM(out.shape, BF16),
        in_specs=[SMEM] + [VMEM] * 3 + [ANY],
        out_specs=ANY,
        scratch_shapes=[
            pltpu.VMEM((longs, tree, heads * LANES), BF16),
            pltpu.SemaphoreType.DMA((longs,)),
        ],
        input_output_aliases={4: 0},
        compiler_params=params(4),
        cost_estimate=estimate(1),
        name="merge",
    )(pair_slot, own_acc, own_sum, back, hbm(out))


def swap(value, axis, mask):
    pairs = [(source, source ^ mask) for source in range(lax.axis_size(axis))]
    return lax.ppermute(value, axis, pairs)


def body(
    hidden,
    norm_gain,
    q_weight,
    k_weight,
    v_weight,
    kv_pages,
    page_table,
    cache_len,
    tree_parent,
    accept_node,
    pair_slot,
    far_len,
    far_table,
    mig_src,
    mig_page,
):
    requests, tree = tree_parent.shape
    token_rows = hidden.shape[0]
    own_pages, page_size, kv_heads, entry = kv_pages.shape
    groups = lax.axis_size("grp")
    me = lax.axis_index("grp")
    spot = lax.axis_index("tp")
    counts = chunk_counts(requests)
    firsts = [sum(counts[:c]) for c in range(len(counts))]
    places = [list(range(f, f + n)) for f, n in zip(firsts, counts, strict=True)]

    order, rank, asked, placed, *rows = order_rows(
        hidden, pair_slot, cache_len, mig_src, mig_page, own_pages, groups, tree, counts
    )
    hidden_core = swap(hidden, "tp", 1)
    from_x = [swap(part, "tp", 2) for part in rows]

    migrations = mig_src.shape[0]
    index = jnp.arange(migrations, dtype=I32)
    wanted = lax.all_to_all(asked, "grp", 0, 0, tiled=True)
    outgoing = pick_pages(kv_pages, wanted)
    from_x[0], _ = lax.optimization_barrier((from_x[0], outgoing))
    from_xc = [swap(part, "tp", 1) for part in from_x]
    incoming = lax.all_to_all(outgoing, "grp", 0, 0, tiled=True)
    moved = incoming.reshape(groups * CAP * page_size, kv_heads * entry)
    held, _ = lax.optimization_barrier((kv_pages, outgoing))
    pool = held.reshape(own_pages * page_size, kv_heads * entry)
    tables = jnp.concatenate([page_table, far_table], 0)
    extra = tables[:, :, None] - own_pages == index[None, None, :]
    tables = jnp.where(
        tables < own_pages, tables, jnp.sum(jnp.where(extra, placed[None, None, :], 0), -1)
    ).reshape(-1)

    parents = tree_parent.reshape(-1, 1)
    half = LANES // 2
    angles = jnp.exp(-THETA_LOG * 2.0 * jnp.arange(half, dtype=F32) / LANES)
    angles = jnp.concatenate([angles, angles])[None, :]
    gain = norm_gain.reshape(-1, hidden.shape[1])
    info = jnp.full((1,), spot, I32)
    far_mine = lax.dynamic_index_in_dim(far_len, me, 0, keepdims=False)
    far_other = lax.dynamic_index_in_dim(far_len, me ^ 1, 0, keepdims=False)

    weights = (q_weight, k_weight, v_weight)
    longs = pair_slot.shape[1]
    scalars = (info, order, rank, cache_len, pair_slot, far_mine, accept_node)
    tables_in = (parents, angles, gain)
    *state, picked0, long_queries = project_first(
        places[0],
        tree,
        longs,
        scalars,
        tables_in,
        weights,
        (hidden, hidden_core, from_x[0], from_xc[0]),
    )
    far_queries = swap(long_queries, "grp", 1)
    out, long_acc, long_sum, far_done = attend_first(
        places[0],
        tree,
        longs,
        requests,
        scalars[1:5],
        far_other,
        tables,
        state,
        far_queries,
        pool,
        moved,
        page_size,
        token_rows,
    )
    back = swap(far_done, "grp", 1)
    out, picked1 = finish(
        places[1],
        tree,
        longs,
        requests,
        scalars,
        tables_in,
        weights,
        (hidden, hidden_core, from_x[1], from_xc[1]),
        tables,
        pool,
        moved,
        page_size,
        out,
    )
    out = merge(tree, pair_slot, long_acc, long_sum, back, out)
    picked = jnp.concatenate([picked0, picked1], 0).reshape(requests, 16, -1)
    accepted = (
        picked[rank, :ACCEPT].reshape(requests * ACCEPT, kv_heads, entry)
    )
    return (out, accepted)


def chunk_counts(requests):
    return (requests // 4, requests - requests // 4)


def solution(mesh):
    in_specs = (
        P("grp", "tp"),
        P(),
        P(None, "tp"),
        P(None, "tp"),
        P(None, "tp"),
        P("grp", None, "tp", None),
        P("grp", None),
        P("grp"),
        P("grp", None),
        P("grp"),
        P("grp", None),
        P(),
        P("grp", None),
        P("grp"),
        P("grp"),
    )
    out_specs = (P("grp", "tp"), P("grp", "tp", None))
    chosen = body if mesh.shape["tp"] == 4 else general_body
    return jax.shard_map(chosen, mesh=mesh, in_specs=in_specs, out_specs=out_specs, check_vma=False)
```

```python
import jax
import jax.numpy as jnp
from jax import lax
from jax.experimental import pallas as pl
from jax.experimental.pallas import tpu as pltpu
from jax.sharding import PartitionSpec as P

D = 4608
CAP = 4
ACCEPT = 5


THETA_LOG = 9.210340371976184
SCORE_SCALE = 144.0 ** (-0.5)
LOGIT_CAP = 50.0
HIGHEST = lax.Precision.HIGHEST
IN_SCALE = SCORE_SCALE / LOGIT_CAP
OUT_SCALE = LOGIT_CAP * 1.4426950408889634
LANES = 128
BLOCK = 256
GROUPED = 4
PAIR = 4
MIB = 2**20
ANY = pl.BlockSpec(memory_space=pl.ANY)
VMEM = pl.BlockSpec(memory_space=pltpu.VMEM)
SMEM = pl.BlockSpec(memory_space=pltpu.SMEM)
BF16 = jnp.bfloat16
F32 = jnp.float32
I32 = jnp.int32


def estimate(micros):
    return pl.CostEstimate(flops=int(micros * 1.15e9), bytes_accessed=0, transcendentals=0)


def params(mib):
    return pltpu.CompilerParams(vmem_limit_bytes=mib * MIB)


def shape(dims, dtype):
    return jax.ShapeDtypeStruct(dims, dtype)


def aligned(index, unit):
    return pl.multiple_of(index * unit, unit)


def partner(value, axis, bit):
    mask = 2**bit
    pairs = [(source, source ^ mask) for source in range(lax.axis_size(axis))]
    return lax.ppermute(value, axis, pairs)


def rotate(values, position):
    halfway = values.shape[-1] // 2
    angles = jnp.exp(-THETA_LOG * 2.0 * jnp.arange(halfway, dtype=jnp.float32) / values.shape[-1])
    phases = position.astype(jnp.float32)[:, None] * angles[None, :]
    cosine = jnp.cos(phases)[:, None, :]
    sine_part = jnp.sin(phases)[:, None, :]
    former = values[..., :halfway]
    latter = values[..., halfway:]
    return jnp.concatenate(
        [former * cosine - latter * sine_part, latter * cosine + former * sine_part], -1
    )


def ancestry(parents):
    length = parents.shape[-1]
    labels = jnp.arange(length, dtype=jnp.int32)
    reached = (parents[..., :, None] == labels).astype(jnp.float32) + jnp.eye(
        length, dtype=jnp.float32
    )
    reached = jnp.minimum(jnp.einsum("nij,njk->nik", reached, reached, precision=HIGHEST), 1.0)
    reached = jnp.minimum(jnp.einsum("nij,njk->nik", reached, reached, precision=HIGHEST), 1.0)
    depths = jnp.sum((reached > 0.5).astype(jnp.int32), -1) - 1
    return (reached, depths)


def absorb(running, queries, keys_block, values_block, allowed):
    largest, summed, weighted = running
    scores = (
        jnp.einsum("igrd,tgd->igrt", queries, keys_block, preferred_element_type=jnp.float32)
        * SCORE_SCALE
    )
    scores = LOGIT_CAP * jnp.tanh(scores / LOGIT_CAP)
    weights = jnp.where(allowed, jnp.exp(scores - LOGIT_CAP), 0.0)
    summed = summed + jnp.sum(weights, -1)
    weighted = weighted + jnp.einsum(
        "igrt,tgd->igrd",
        weights.astype(jnp.bfloat16),
        values_block,
        preferred_element_type=jnp.float32,
    )
    return (largest, summed, weighted)


def empty_state(queries):
    leading = queries.shape[:3]
    return (
        jnp.full(leading, LOGIT_CAP, jnp.float32),
        jnp.zeros(leading, jnp.float32),
        jnp.zeros(queries.shape, jnp.float32),
    )


def attend_blocks(queries, loader, length, block_span):
    turns = (length + block_span - 1) // block_span

    def advance(number, running):
        keys_block, values_block = loader(number)
        allowed = (number * block_span + jnp.arange(block_span, dtype=jnp.int32) < length)[
            None, None, None, :
        ]
        return absorb(running, queries, keys_block, values_block, allowed)

    return lax.fori_loop(0, turns, advance, empty_state(queries))


def combine(states):
    summed = jnp.zeros(states[0][1].shape, jnp.float32)
    weighted = jnp.zeros(states[0][2].shape, jnp.float32)
    for state in states:
        summed = summed + state[1]
        weighted = weighted + state[2]
    return weighted / summed[..., None]


def general_body(
    hidden,
    norm_gain,
    q_weight,
    k_weight,
    v_weight,
    kv_pages,
    page_table,
    cache_len,
    tree_parent,
    accept_node,
    pair_slot,
    far_len,
    far_table,
    mig_src,
    mig_page,
):
    token_rows = hidden.shape[0]
    requests = cache_len.shape[0]
    tree_size = tree_parent.shape[1]
    head_size = kv_pages.shape[3] // 2
    local_heads = kv_pages.shape[2]
    page_size = kv_pages.shape[1]
    table_width = page_table.shape[1]
    long_count = pair_slot.shape[1]
    migrations = mig_src.shape[0]
    groups = lax.axis_size("grp")
    myself = lax.axis_index("grp")
    widened = lax.all_gather(hidden, "tp", axis=1, tiled=True).astype(jnp.float32)
    scaled = (widened * norm_gain[None, :]).astype(jnp.bfloat16)
    query_sum = jnp.dot(scaled, q_weight, preferred_element_type=jnp.float32)
    key_sum = jnp.dot(scaled, k_weight, preferred_element_type=jnp.float32)
    value_sum = jnp.dot(scaled, v_weight, preferred_element_type=jnp.float32)
    squares = jnp.sum(widened * widened, 1)
    query_sum, key_sum, value_sum, squares = (query_sum, key_sum, value_sum, squares)
    row_scale = lax.rsqrt(squares / D + 1e-06)[:, None]
    reached, depths = ancestry(tree_parent)
    far_mine = lax.dynamic_index_in_dim(far_len, myself, 0, keepdims=False)
    long_slots = pair_slot[0]
    matched = jnp.arange(requests, dtype=jnp.int32)[:, None] == long_slots[None, :]
    far_own = jnp.sum(jnp.where(matched, far_mine[None, :], 0), 1)
    position = ((cache_len + far_own)[:, None] + depths).reshape(-1)
    queries = rotate(
        (query_sum * row_scale).reshape(token_rows, 2 * local_heads, head_size), position
    ).astype(jnp.bfloat16)
    keys_new = rotate(
        (key_sum * row_scale).reshape(token_rows, local_heads, head_size), position
    ).astype(jnp.bfloat16)
    values_new = (
        (value_sum * row_scale).astype(jnp.bfloat16).reshape(token_rows, local_heads, head_size)
    )
    order_index = jnp.arange(migrations, dtype=jnp.int32)
    earlier = order_index[:, None] > order_index[None, :]

    def rank_of(sources):
        return jnp.sum(
            ((sources[..., :, None] == sources[..., None, :]) & earlier).astype(jnp.int32), -1
        )

    own_rank = rank_of(mig_src)
    slot_index = jnp.arange(CAP, dtype=jnp.int32)
    every_source, every_page = (
        lax.all_gather(mig_src, "grp", axis=0, tiled=True),
        lax.all_gather(mig_page, "grp", axis=0, tiled=True),
    )
    every_source = every_source.reshape(groups, migrations)
    every_page = every_page.reshape(groups, migrations)
    every_rank = rank_of(every_source)
    hits = (every_source[:, :, None] == myself) & (
        every_rank[:, :, None] == slot_index[None, None, :]
    )
    wanted = jnp.sum(jnp.where(hits, every_page[:, :, None] + 1, 0), 1) - 1
    present = (wanted >= 0)[:, :, None, None, None]
    outgoing = jnp.where(present, kv_pages[jnp.maximum(wanted, 0)], jnp.zeros((), jnp.bfloat16))
    incoming = lax.all_to_all(outgoing, "grp", split_axis=0, concat_axis=0, tiled=True)
    moved = incoming.reshape(groups * CAP, page_size, local_heads, 2 * head_size)[
        mig_src * CAP + own_rank
    ]
    extended = jnp.concatenate([kv_pages, moved], 0)
    block_pages = min(32, table_width)
    block_span = block_pages * page_size

    def page_loader(table_row):

        def loader(number):
            chosen = lax.dynamic_slice_in_dim(table_row, number * block_pages, block_pages, 0)
            gathered = extended[chosen].reshape(block_span, local_heads, 2 * head_size)
            return (gathered[..., :head_size], gathered[..., head_size:])

        return loader

    grouped = queries.reshape(requests, tree_size, local_heads, 2, head_size)
    long_queries = grouped[long_slots]
    far_dense = extended[far_table].reshape(
        long_count, table_width * page_size, local_heads, 2 * head_size
    )
    arrived = partner(far_dense, "grp", 0)

    def owner_part(packed):
        query_block, cache_block, length = packed

        def loader(number):
            portion = lax.dynamic_slice_in_dim(cache_block, number * block_span, block_span, 0)
            return (portion[..., :head_size], portion[..., head_size:])

        return attend_blocks(query_block, loader, length, block_span)

    far_parts = lax.map(owner_part, (long_queries, arrived, far_mine))
    keys_grouped = keys_new.reshape(requests, tree_size, local_heads, head_size)
    values_grouped = values_new.reshape(requests, tree_size, local_heads, head_size)

    def request_part(packed):
        query_block, key_block, value_block, table_row, length, tree_mask, match_row = packed
        own_state = attend_blocks(query_block, page_loader(table_row), length, block_span)
        tree_state = absorb(
            empty_state(query_block),
            query_block,
            key_block,
            value_block,
            (tree_mask > 0.5)[:, None, None, :],
        )
        chooser = match_row[:, None, None, None]
        far_state = (
            own_state[0],
            jnp.sum(jnp.where(chooser, far_parts[1], 0.0), 0),
            jnp.sum(jnp.where(match_row[:, None, None, None, None], far_parts[2], 0.0), 0),
        )
        mixed = combine((own_state, tree_state, far_state))
        return mixed.reshape(tree_size, 2 * local_heads * head_size).astype(jnp.bfloat16)

    attn_out = lax.map(
        request_part,
        (grouped, keys_grouped, values_grouped, page_table, cache_len, reached, matched),
    ).reshape(token_rows, 2 * local_heads * head_size)
    leaves = (jnp.arange(tree_size, dtype=jnp.int32)[None, :] == accept_node[:, None]).astype(
        jnp.float32
    )
    lineage = jnp.einsum("rt,rtj->rj", leaves, reached, precision=HIGHEST)
    levels = (depths[:, None, :] == jnp.arange(ACCEPT, dtype=jnp.int32)[None, :, None]).astype(
        jnp.float32
    )
    picker = lineage[:, None, :] * levels
    fresh_rows = (
        jnp.concatenate([keys_new, values_new], -1)
        .reshape(requests, tree_size, local_heads * 2 * head_size)
        .astype(jnp.float32)
    )
    accepted = (
        jnp.einsum("rpt,rtc->rpc", picker, fresh_rows, precision=HIGHEST)
        .astype(jnp.bfloat16)
        .reshape(requests * ACCEPT, local_heads, 2 * head_size)
    )
    return (attn_out, accepted)


def order_rows(hidden, pair_slot, cache_len, mig_src, mig_page, own_pages, groups, tree_size, counts):
    requests, longs = cache_len.shape[0], pair_slot.shape[1]
    migrations = mig_src.shape[0]
    width = hidden.shape[1]

    def kernel(
        pair_ref, length_ref, source_ref, page_ref, hidden_ref, order_ref, rank_ref, asked, placed, *outs
    ):
        taken = [jnp.int32(0)] * migrations
        for i in range(migrations):
            for j in range(i):
                taken[i] = taken[i] + (source_ref[i] == source_ref[j]).astype(I32)
        for i in range(groups):
            for j in range(CAP):
                asked[i, j] = jnp.int32(0)
        for i in range(migrations):
            asked[source_ref[i], taken[i]] = page_ref[i]
            placed[i] = own_pages + source_ref[i] * CAP + taken[i]
        weight = []
        for i in range(requests):
            value = length_ref[i]
            for j in range(longs):
                value = value + jnp.where(pair_ref[0, j] == i, 1 << 20, 0)
            weight.append(value)
        ranks = [jnp.int32(0)] * requests
        for i in range(requests):
            for j in range(i):
                ahead = (weight[j] >= weight[i]).astype(I32)
                ranks[i] = ranks[i] + ahead
                ranks[j] = ranks[j] + 1 - ahead
        for i in range(requests):
            order_ref[ranks[i]] = jnp.int32(i)
            rank_ref[i] = ranks[i]
        place = 0
        for out, count in zip(outs, counts, strict=True):
            for i in range(count):
                out[pl.ds(i * tree_size, tree_size), :] = hidden_ref[
                    pl.ds(aligned(order_ref[place], tree_size), tree_size), :
                ]
                place += 1

    return pl.pallas_call(
        kernel,
        out_shape=[
            *[shape((requests,), I32)] * 2,
            shape((groups, CAP), I32),
            shape((migrations,), I32),
            *[shape((count * tree_size, width), BF16) for count in counts],
        ],
        in_specs=[SMEM] * 4 + [VMEM],
        out_specs=[SMEM] * 4 + [VMEM] * len(counts),
        cost_estimate=estimate(2),
        compiler_params=params(8),
        name="order_rows",
    )(*[hbm(a) for a in (pair_slot, cache_len, mig_src, mig_page)], hidden)


def pick_pages(pages, wanted):
    peers, slots = wanted.shape

    def kernel(wanted_ref, pages_ref, out, sem):
        copies = []
        for peer in range(peers):
            for slot in range(slots):
                copies.append(
                    pltpu.make_async_copy(
                        pages_ref.at[wanted_ref[peer, slot]],
                        out.at[peer, slot],
                        sem.at[peer * slots + slot],
                    )
                )
                copies[-1].start()
        for copy in copies:
            copy.wait()

    return pl.pallas_call(
        kernel,
        out_shape=shape((peers, slots, *pages.shape[1:]), BF16),
        in_specs=[SMEM, ANY],
        out_specs=VMEM,
        scratch_shapes=[pltpu.SemaphoreType.DMA((peers * slots,))],
        cost_estimate=estimate(1.5),
        compiler_params=params(4),
        name="pick_pages",
    )(wanted, hbm(pages))


def project_core(places, tree, longs, depth_all, info, inputs, scratch, q_ref, acc_ref, sum_ref, picked_out, long_out, started=lambda: None):
    (info_ref, order_ref, rank_ref, length_ref, pair_ref, far_ref, accept_ref) = info
    (parents_ref, angles_ref, gain_ref, *weight_refs, own_ref, core_ref, x_ref, xc_ref) = inputs
    (blocks, reached_ref, *kept, q_sum, k_sum, v_sum, square_sum, sem, weight_sem) = scratch
    totals = (q_sum, k_sum, v_sum)
    count = len(places)
    paired = PAIR * tree
    padded = -(-paired // LANES) * LANES
    filler = padded - paired
    quarter = blocks.shape[2]
    heads = kept[0].shape[1] // LANES
    kv_heads = kept[1].shape[1] // LANES
    share = heads // kv_heads
    per_item = heads * tree
    requests = [order_ref[place] for place in places]
    me = info_ref[0]
    loads = []
    for part in range(4):
        span = pl.ds(aligned(me ^ part, quarter), quarter)
        if part < 2:
            source = (own_ref, core_ref)[part]
            for i, request in enumerate(requests):
                loads.append(
                    pltpu.make_async_copy(
                        source.at[pl.ds(aligned(request, tree), tree)],
                        blocks.at[part, pl.ds(i * tree, tree)],
                        sem.at[part],
                    )
                )
        else:
            source = (x_ref, xc_ref)[part - 2]
            loads.append(pltpu.make_async_copy(source, blocks.at[part], sem.at[part]))
        for number, (source, target) in enumerate(zip(weight_refs, kept, strict=True)):
            loads.append(
                pltpu.make_async_copy(
                    source.at[span], target.at[span], weight_sem.at[part, number]
                )
            )
    for load in loads:
        load.start()
    started()
    labels = lax.broadcasted_iota(I32, (padded, padded), 1)
    mine = lax.broadcasted_iota(I32, (padded, padded), 0)
    reached, depth_columns, depth_rows = [], [], []
    for p in range(count // PAIR):
        column = []
        for i in range(PAIR):
            part = parents_ref[pl.ds(aligned(requests[p * PAIR + i], tree), tree), :]
            column.append(jnp.where(part < 0, -1, part + i * tree))
        column = jnp.concatenate([*column, jnp.full((filler, 1), -1, I32)], 0)
        step = ((column == labels) | (mine == labels)).astype(F32).astype(BF16)
        step = jnp.minimum(jnp.dot(step, step, preferred_element_type=F32), 1.0).astype(BF16)
        whole = jnp.minimum(jnp.dot(step, step, preferred_element_type=F32), 1.0)
        reached_ref[p * padded : (p + 1) * padded, :] = whole
        reached.append(whole[:paired])
        depth_columns.append(jnp.sum(whole[:paired], 1, keepdims=True) - 1.0)
        depth_rows.append(
            lax.dot_general(
                jnp.ones((16, padded), BF16),
                whole.astype(BF16),
                (((1,), (1,)), ((), ())),
                preferred_element_type=F32,
            )
            - 1.0
        )
    bases = []
    for request in requests:
        base = length_ref[request]
        for j in range(longs):
            base = base + jnp.where(pair_ref[0, j] == request, far_ref[j], 0)
        bases.append(jnp.full((tree, 1), base, I32))
    position = jnp.concatenate(bases, 0).astype(F32) + jnp.concatenate(depth_columns, 0)
    phases = position * angles_ref[...]
    cosine = jnp.cos(phases)
    half = LANES // 2
    sign = jnp.where(lax.broadcasted_iota(I32, (1, LANES), 1) < half, -1.0, 1.0)
    sine = jnp.sin(phases) * sign
    square_sum[...] = jnp.zeros_like(square_sum)
    for total in totals:
        total[...] = jnp.zeros_like(total)

    def part_step(part, carried):
        which = me ^ part
        span = pl.ds(aligned(which, quarter), quarter)
        pltpu.make_async_copy(x_ref, blocks.at[part], sem.at[part]).wait()
        for number, (source, target) in enumerate(zip(weight_refs, kept, strict=True)):
            pltpu.make_async_copy(
                source.at[span], target.at[span], weight_sem.at[part, number]
            ).wait()
        wide = blocks[part].astype(F32)
        square = wide * wide
        folded = square[:, :LANES]
        for c in range(1, quarter // LANES):
            folded = folded + square[:, c * LANES : (c + 1) * LANES]
        square_sum[...] += folded
        scaled = (wide * gain_ref[pl.ds(which, 1), :]).astype(BF16)
        for ref, total in zip(kept, totals, strict=True):
            total[...] += jnp.dot(scaled, ref[span, :], preferred_element_type=F32)
        return carried

    lax.fori_loop(0, 4, part_step, 0)
    sums = [total[...] for total in totals]
    squares = jnp.sum(square_sum[...], 1, keepdims=True)
    row_scale = lax.rsqrt(squares / depth_all + 1e-06)

    def rope(values):
        return (values * cosine + pltpu.roll(values, half, 1) * sine).astype(BF16)

    def head_of(values, h):
        return values[:, h * LANES : (h + 1) * LANES] * row_scale

    keys = [rope(head_of(sums[1], g)) for g in range(kv_heads)]
    values = [head_of(sums[2], g).astype(BF16) for g in range(kv_heads)]

    def pad(block):
        return jnp.concatenate([block, jnp.zeros((filler, LANES), BF16)], 0)

    queries = [rope(head_of(sums[0], h)) for h in range(heads)]
    zeros = jnp.zeros((tree, LANES), BF16)
    levels = lax.broadcasted_iota(I32, (16, padded), 0).astype(F32)
    pairs = range(count // PAIR)
    cuts = [slice(p * paired, (p + 1) * paired) for p in pairs]
    pair_keys = [[pad(block[cut]) for block in keys] for cut in cuts]
    pair_values = [[pad(block[cut]) for block in values] for cut in cuts]
    each = [(p, g) for p in pairs for g in range(kv_heads)]
    scores = [
        lax.dot_general(
            jnp.concatenate([queries[g * share + r][cuts[p]] for r in range(share)], 0),
            pair_keys[p][g],
            (((1,), (1,)), ((), ())),
            preferred_element_type=F32,
        )
        for p, g in each
    ]
    masks = [jnp.concatenate([block] * share, 0) for block in reached]
    exped = [
        jnp.exp2(jnp.tanh(score * IN_SCALE) * OUT_SCALE) * masks[p]
        for (p, g), score in zip(each, scores, strict=True)
    ]
    mixed = [
        jnp.dot(block.astype(BF16), pair_values[p][g], preferred_element_type=F32)
        for (p, g), block in zip(each, exped, strict=True)
    ]
    pickers = []
    for p in pairs:
        picks = []
        for i in range(PAIR):
            leaf = accept_ref[requests[p * PAIR + i]] + p * padded + i * tree
            picks.append(jnp.where(depth_rows[p] == levels, reached_ref[pl.ds(leaf, 1), :], 0.0))
        pickers.append(jnp.concatenate(picks, 0).astype(BF16))
    picked = []
    for p in pairs:
        fresh = [block for g in range(kv_heads) for block in (pair_keys[p][g], pair_values[p][g])]
        picked.append(
            jnp.dot(pickers[p], jnp.concatenate(fresh, 1), preferred_element_type=F32)
        )
    for (p, g), block, weight in zip(each, mixed, exped, strict=True):
        total = weight[:, :LANES]
        for c in range(1, padded // LANES):
            total = total + weight[:, c * LANES : (c + 1) * LANES]
        for r in range(share):
            h = g * share + r
            for i in range(PAIR):
                start = (p * PAIR + i) * per_item + h * tree
                there = slice(start, start + tree)
                inside = slice(r * paired + i * tree, r * paired + (i + 1) * tree)
                acc_ref[there, :] = block[inside]
                sum_ref[there, :] = total[inside]
                first = p * paired + i * tree
                for other in range(kv_heads):
                    q_ref[there, other * LANES : (other + 1) * LANES] = (
                        queries[h][first : first + tree] if other == g else zeros
                    )
    for p in pairs:
        picked_out[p * PAIR * 16 : (p + 1) * PAIR * 16, :] = picked[p].astype(BF16)
    if long_out is not None:
        for j in range(longs):
            place = rank_ref[pair_ref[0, j]]
            long_out[j * per_item : (j + 1) * per_item, :] = q_ref[
                pl.ds(aligned(place, per_item), per_item), :
            ]


def project_scratch(count, tree, hidden, weights):
    padded = -(-PAIR * tree // LANES) * LANES
    return [
        pltpu.VMEM((4, count * tree, hidden.shape[1]), BF16),
        pltpu.VMEM((count // PAIR * padded, padded), F32),
        *[pltpu.VMEM(weight.shape, BF16) for weight in weights],
        *[pltpu.VMEM((count * tree, weight.shape[1]), F32) for weight in weights],
        pltpu.VMEM((count * tree, LANES), F32),
        pltpu.SemaphoreType.DMA((4,)),
        pltpu.SemaphoreType.DMA((4, len(weights))),
    ]


def state_scratch(count, per_item, width):
    return [
        pltpu.VMEM((count * per_item, width), BF16),
        pltpu.VMEM((count * per_item, LANES), F32),
        pltpu.VMEM((count * per_item, LANES), F32),
    ]


def hbm(array):
    return pltpu.with_memory_space_constraint(array, pltpu.HBM)


def project_first(places, tree, longs, scalars, tables, weights, parts):
    count = len(places)
    hidden = parts[0]
    heads = weights[0].shape[1] // LANES
    width = weights[1].shape[1]
    per_item = heads * tree
    depth_all = weights[0].shape[0]
    n_scratch = len(project_scratch(count, tree, hidden, weights))

    def kernel(*refs):
        info, refs = refs[:7], refs[7:]
        inputs, refs = refs[:10], refs[10:]
        outs, (picked_out, long_out), refs = refs[:3], refs[3:5], refs[5:]
        state, scratch, sem = refs[:3], refs[3 : 3 + n_scratch], refs[-1]
        project_core(
            places, tree, longs, depth_all, info, inputs, scratch, *state, picked_out, long_out
        )
        copies = [
            pltpu.make_async_copy(source, target, sem.at[i])
            for i, (source, target) in enumerate(zip(state, outs, strict=True))
        ]
        for copy in copies:
            copy.start()
        for copy in copies:
            copy.wait()

    rows = count * per_item
    return pl.pallas_call(
        kernel,
        out_shape=[
            pltpu.HBM((rows, width), BF16),
            pltpu.HBM((rows, LANES), F32),
            pltpu.HBM((rows, LANES), F32),
            shape((count * 16, 2 * width), BF16),
            shape((longs * per_item, width), BF16),
        ],
        in_specs=[SMEM] * 7 + [VMEM] * 3 + [ANY] * 7,
        out_specs=[ANY] * 3 + [VMEM] * 2,
        scratch_shapes=[
            *state_scratch(count, per_item, width),
            *project_scratch(count, tree, hidden, weights),
            pltpu.SemaphoreType.DMA((3,)),
        ],
        compiler_params=params(40),
        cost_estimate=estimate(1),
        name="project_first",
    )(*scalars, *tables, *[hbm(a) for a in (*weights, *parts[:2])], *parts[2:])


def attend_core(lens, rows_of, table_ref, cache, qs, acc, sums, score_refs, weight_refs, page_size):
    count = lens.shape[0]
    width = qs.shape[1]
    kv_heads = width // LANES
    per_item = qs.shape[0] // count
    half = per_item // kv_heads
    pages = BLOCK // page_size
    blocks = jnp.int32(0)
    for i in range(count):
        blocks = blocks + (lens[i] + BLOCK - 1) // BLOCK
    def following(state):
        item, block = state
        last = (block + 1) * BLOCK >= lens[item]
        return (
            jnp.where(last, jnp.minimum(item + 1, count - 1), item),
            jnp.where(last, 0, block + 1),
        )

    def gathered(state, first):
        item, block = state
        base = rows_of[item] + block * pages
        spans = [
            pl.ds(aligned(table_ref[base + j], page_size), page_size) for j in range(pages)
        ]
        sides = []
        for g in range(kv_heads):
            lanes = slice((2 * g + first) * LANES, (2 * g + first + 1) * LANES)
            sides.append(jnp.concatenate([cache[span, lanes] for span in spans], 0))
        return jnp.concatenate(sides, 1)

    def score(state, scores):
        item = state[0]
        scores[...] = lax.dot_general(
            qs[pl.ds(aligned(item, per_item), per_item), :],
            gathered(state, 0),
            (((1,), (1,)), ((), ())),
            preferred_element_type=F32,
        )

    def weigh(state, number, scores, weights):
        item, block = state
        left = jnp.where(number < blocks, lens[item] - block * BLOCK, 0)
        allowed = lax.broadcasted_iota(I32, (1, BLOCK), 1) < left
        exped = jnp.exp2(jnp.tanh(scores[...] * IN_SCALE) * OUT_SCALE)
        exped = jnp.where(allowed, exped, 0.0)
        weights[...] = exped.astype(BF16)
        part = exped[:, :LANES]
        for c in range(1, BLOCK // LANES):
            part = part + exped[:, c * LANES : (c + 1) * LANES]
        sums[pl.ds(aligned(item, per_item), per_item), :] += part

    def mix(state, weights):
        item = state[0]
        mixed = jnp.dot(
            weights[...], gathered(state, 1), preferred_element_type=F32
        )
        for g in range(kv_heads):
            there = pl.ds(aligned(item * kv_heads + g, half), half)
            acc[there, :] += mixed[
                g * half : (g + 1) * half, g * LANES : (g + 1) * LANES
            ]

    def group_from(state):
        states = [state]
        for _ in range(GROUPED - 1):
            states.append(following(states[-1]))
        return states, following(states[-1])

    group0, next0 = group_from((jnp.int32(0), jnp.int32(0)))
    for u in range(GROUPED):
        score(group0[u], score_refs[u])
    for u in range(GROUPED):
        weigh(group0[u], u, score_refs[u], weight_refs[u])
    group1, next1 = group_from(next0)
    for u in range(GROUPED):
        score(group1[u], score_refs[u])

    def turn(number, carried):
        state0, state1, state2 = carried
        now0, _ = group_from(state0)
        now1, _ = group_from(state1)
        now2, state3 = group_from(state2)
        for u in range(GROUPED):
            mix(now0[u], weight_refs[u])
            weigh(now1[u], (number + 1) * GROUPED + u, score_refs[u], weight_refs[u])
            score(now2[u], score_refs[u])
        return state1, state2, state3

    lax.fori_loop(
        0,
        (blocks + GROUPED - 1) // GROUPED,
        turn,
        ((jnp.int32(0), jnp.int32(0)), next0, next1),
    )


def attend_scratch(count, per_item, cache_rows, cache_width):
    return [
        pltpu.VMEM((cache_rows, cache_width), BF16),
        pltpu.SMEM((count,), I32),
        pltpu.SMEM((count,), I32),
        *[pltpu.VMEM((per_item, BLOCK), F32) for _ in range(GROUPED)],
        *[pltpu.VMEM((per_item, BLOCK), BF16) for _ in range(GROUPED)],
    ]


def lay(target, block, tree):
    for h in range(block.shape[0] // tree):
        target[:, h * LANES : (h + 1) * LANES] = block[h * tree : (h + 1) * tree].astype(
            BF16
        )


def bring_cache(pool_ref, moved_ref, cache, sem):
    rows = pool_ref.shape[0]
    quarter = rows // 4
    copies = [
        pltpu.make_async_copy(
            pool_ref.at[pl.ds(c * quarter, quarter)],
            cache.at[pl.ds(c * quarter, quarter)],
            sem.at[c],
        )
        for c in range(4)
    ]
    copies.append(
        pltpu.make_async_copy(moved_ref, cache.at[pl.ds(rows, moved_ref.shape[0])], sem.at[4])
    )
    for copy in copies:
        copy.start()
    return copies


def send_out(number, request, staged, out_ref, sem, tree):
    copy = pltpu.make_async_copy(
        staged.at[number], out_ref.at[pl.ds(aligned(request, tree), tree)], sem.at[number]
    )
    copy.start()
    return copy


def attend_first(
    places, tree, longs, requests, scalars, far_len, table, state, far_queries, pool, moved, page_size, token_rows
):
    own = len(places)
    count = own + longs
    rows, width = state[0].shape
    per_item = rows // own
    heads = per_item // tree
    far_rows = longs * per_item
    table_width = table.shape[0] // (requests + longs)
    cache_rows, cache_width = pool.shape[0] + moved.shape[0], pool.shape[1]

    def kernel(*refs):
        (order_ref, rank_ref, length_ref, pair_ref, far_ref, table_ref), refs = refs[:6], refs[6:]
        state_refs, (far_q, pool_ref, moved_ref), refs = refs[:3], refs[3:6], refs[6:]
        (out_ref, long_acc, long_sum, far_out), refs = refs[:4], refs[4:]
        (qs, acc, sums), (staged, sem, cache_sem), refs = refs[:3], refs[3:6], refs[6:]
        (cache, lens, rows_of), refs = refs[:3], refs[3:]
        copies = bring_cache(pool_ref, moved_ref, cache, cache_sem)
        for i, (source, target) in enumerate(zip(state_refs, (qs, acc, sums), strict=True)):
            copies.append(pltpu.make_async_copy(source, target.at[pl.ds(0, rows)], sem.at[i]))
            copies[-1].start()
        copies.append(pltpu.make_async_copy(far_q, qs.at[pl.ds(rows, far_rows)], sem.at[3]))
        copies[-1].start()
        acc[rows:, :] = jnp.zeros((far_rows, LANES), F32)
        sums[rows:, :] = jnp.zeros((far_rows, LANES), F32)
        for i, place in enumerate(places):
            request = order_ref[place]
            lens[i] = length_ref[request]
            rows_of[i] = request * table_width
        for j in range(longs):
            lens[own + j] = far_ref[j]
            rows_of[own + j] = (requests + j) * table_width
        for copy in copies:
            copy.wait()
        attend_core(
            lens, rows_of, table_ref, cache, qs, acc, sums, refs[:GROUPED], refs[GROUPED:], page_size
        )
        total = jnp.sum(sums[rows:, :], 1, keepdims=True)
        far_out[:, :LANES] = acc[rows:, :].astype(BF16)
        far_out[:, LANES:] = jnp.broadcast_to(total, (far_rows, LANES)).astype(BF16)
        sent = []
        for i, place in enumerate(places):
            there = slice(i * per_item, (i + 1) * per_item)
            lay(staged.at[i], acc[there, :] / jnp.sum(sums[there, :], 1, keepdims=True), tree)
            sent.append(send_out(i, order_ref[place], staged, out_ref, sem, tree))
        for j in range(longs):
            there = slice(j * per_item, (j + 1) * per_item)
            here = pl.ds(aligned(rank_ref[pair_ref[0, j]], per_item), per_item)
            long_acc[there, :] = acc[here, :]
            long_sum[there, :] = sums[here, :]
        for copy in sent:
            copy.wait()

    return pl.pallas_call(
        kernel,
        out_shape=[
            pltpu.HBM((token_rows, heads * LANES), BF16),
            shape((far_rows, LANES), F32),
            shape((far_rows, LANES), F32),
            shape((far_rows, 2 * LANES), BF16),
        ],
        in_specs=[SMEM] * 6 + [ANY] * 6,
        out_specs=[ANY] + [VMEM] * 3,
        scratch_shapes=[
            *state_scratch(count, per_item, width),
            pltpu.VMEM((own, tree, heads * LANES), BF16),
            pltpu.SemaphoreType.DMA((max(own, 4),)),
            pltpu.SemaphoreType.DMA((5,)),
            *attend_scratch(count, per_item, cache_rows, cache_width),
        ],
        compiler_params=params(32),
        cost_estimate=estimate(18),
        name="attend_first",
    )(*scalars, far_len, table, *[hbm(a) for a in state], far_queries, hbm(pool), hbm(moved))


def finish(
    places, tree, longs, requests, scalars, tables, weights, parts, table, pool, moved, page_size, out
):
    own = len(places)
    hidden = parts[0]
    heads = weights[0].shape[1] // LANES
    width = weights[1].shape[1]
    per_item = heads * tree
    depth_all = weights[0].shape[0]
    n_scratch = len(project_scratch(own, tree, hidden, weights))
    table_width = table.shape[0] // (requests + longs)
    cache_rows, cache_width = pool.shape[0] + moved.shape[0], pool.shape[1]

    def kernel(*refs):
        info, table_ref, refs = refs[:7], refs[7], refs[8:]
        order_ref, length_ref = info[1], info[3]
        inputs, refs = refs[:10], refs[10:]
        (pool_ref, moved_ref), refs = refs[:2], refs[3:]
        (out_ref, picked_out), refs = refs[:2], refs[2:]
        (qs, acc, sums), (staged, sem, cache_sem), refs = refs[:3], refs[3:6], refs[6:]
        scratch, refs = refs[:n_scratch], refs[n_scratch:]
        (cache, lens, rows_of), refs = refs[:3], refs[3:]
        for i, place in enumerate(places):
            request = order_ref[place]
            lens[i] = length_ref[request]
            rows_of[i] = request * table_width
        copies = []
        project_core(
            places, tree, longs, depth_all, info, inputs, scratch, qs, acc, sums, picked_out, None,
            lambda: copies.extend(bring_cache(pool_ref, moved_ref, cache, cache_sem)),
        )

        @pl.when(info[0][0] >= 0)
        def _():
            for copy in copies:
                copy.wait()

        attend_core(
            lens, rows_of, table_ref, cache, qs, acc, sums, refs[:GROUPED], refs[GROUPED:], page_size
        )
        sent = []
        for i, place in enumerate(places):
            there = slice(i * per_item, (i + 1) * per_item)
            lay(staged.at[i], acc[there, :] / jnp.sum(sums[there, :], 1, keepdims=True), tree)
            sent.append(send_out(i, order_ref[place], staged, out_ref, sem, tree))
        for copy in sent:
            copy.wait()

    operands = [*scalars, table, *tables]
    operands += [hbm(a) for a in (*weights, *parts[:2])]
    operands += [*parts[2:], *[hbm(a) for a in (pool, moved, out)]]
    return pl.pallas_call(
        kernel,
        out_shape=[pltpu.HBM(out.shape, BF16), shape((own * 16, 2 * width), BF16)],
        in_specs=[SMEM] * 8 + [VMEM] * 3 + [ANY] * 10,
        out_specs=[ANY, VMEM],
        scratch_shapes=[
            *state_scratch(own, per_item, width),
            pltpu.VMEM((own, tree, heads * LANES), BF16),
            pltpu.SemaphoreType.DMA((own,)),
            pltpu.SemaphoreType.DMA((5,)),
            *project_scratch(own, tree, hidden, weights),
            *attend_scratch(own, per_item, cache_rows, cache_width),
        ],
        input_output_aliases={len(operands) - 1: 0},
        compiler_params=params(48),
        cost_estimate=estimate(18),
        name="finish",
    )(*operands)


def merge(tree, pair_slot, rank, own_acc, own_sum, back, picked, out):
    requests = rank.shape[0]
    kv_heads = picked[0].shape[1] // (2 * LANES)
    ends = [0, picked[0].shape[0], picked[0].shape[0] + picked[1].shape[0]]
    longs = pair_slot.shape[1]
    per_item = own_acc.shape[0] // longs
    heads = per_item // tree

    def kernel(
        pair_ref, rank_ref, acc_ref, sum_ref, back_ref, first, second, _, out_ref, accepted, staged, every, sem
    ):
        sent = []
        for j in range(longs):
            there = slice(j * per_item, (j + 1) * per_item)
            total = jnp.sum(sum_ref[there, :], 1, keepdims=True)
            total = total + back_ref[there, LANES : 2 * LANES].astype(F32)
            whole = acc_ref[there, :] + back_ref[there, :LANES].astype(F32)
            lay(staged.at[j], whole / total, tree)
            sent.append(send_out(j, pair_ref[0, j], staged, out_ref, sem, tree))
        every[ends[0] : ends[1], :] = first[...]
        every[ends[1] : ends[2], :] = second[...]
        for r in range(requests):
            path = every[pl.ds(aligned(rank_ref[r], 16), 16), :]
            for g in range(kv_heads):
                accepted[r * ACCEPT : (r + 1) * ACCEPT, g, :] = path[
                    :ACCEPT, 2 * g * LANES : 2 * (g + 1) * LANES
                ]
        for copy in sent:
            copy.wait()

    return pl.pallas_call(
        kernel,
        out_shape=[
            pltpu.HBM(out.shape, BF16),
            shape((requests * ACCEPT, kv_heads, 2 * LANES), BF16),
        ],
        in_specs=[SMEM] * 2 + [VMEM] * 5 + [ANY],
        out_specs=[ANY, VMEM],
        scratch_shapes=[
            pltpu.VMEM((longs, tree, heads * LANES), BF16),
            pltpu.VMEM((ends[2], picked[0].shape[1]), BF16),
            pltpu.SemaphoreType.DMA((longs,)),
        ],
        input_output_aliases={7: 0},
        compiler_params=params(4),
        cost_estimate=estimate(1),
        name="merge",
    )(pair_slot, rank, own_acc, own_sum, back, *picked, hbm(out))


def swap(value, axis, mask):
    pairs = [(source, source ^ mask) for source in range(lax.axis_size(axis))]
    return lax.ppermute(value, axis, pairs)


def body(
    hidden,
    norm_gain,
    q_weight,
    k_weight,
    v_weight,
    kv_pages,
    page_table,
    cache_len,
    tree_parent,
    accept_node,
    pair_slot,
    far_len,
    far_table,
    mig_src,
    mig_page,
):
    requests, tree = tree_parent.shape
    token_rows = hidden.shape[0]
    own_pages, page_size, kv_heads, entry = kv_pages.shape
    groups = lax.axis_size("grp")
    me = lax.axis_index("grp")
    spot = lax.axis_index("tp")
    counts = chunk_counts(requests)
    firsts = [sum(counts[:c]) for c in range(len(counts))]
    places = [list(range(f, f + n)) for f, n in zip(firsts, counts, strict=True)]

    order, rank, asked, placed, *rows = order_rows(
        hidden, pair_slot, cache_len, mig_src, mig_page, own_pages, groups, tree, counts
    )
    hidden_core = swap(hidden, "tp", 1)
    from_x = [swap(part, "tp", 2) for part in rows]

    migrations = mig_src.shape[0]
    index = jnp.arange(migrations, dtype=I32)
    wanted = lax.all_to_all(asked, "grp", 0, 0, tiled=True)
    outgoing = pick_pages(kv_pages, wanted)
    outgoing, from_x[0] = lax.optimization_barrier((outgoing, from_x[0]))
    from_xc = [swap(part, "tp", 1) for part in from_x]
    incoming = lax.all_to_all(outgoing, "grp", 0, 0, tiled=True)
    moved = incoming.reshape(groups * CAP * page_size, kv_heads * entry)
    held, _ = lax.optimization_barrier((kv_pages, outgoing))
    pool = held.reshape(own_pages * page_size, kv_heads * entry)
    tables = jnp.concatenate([page_table, far_table], 0)
    extra = tables[:, :, None] - own_pages == index[None, None, :]
    tables = jnp.where(
        tables < own_pages, tables, jnp.sum(jnp.where(extra, placed[None, None, :], 0), -1)
    ).reshape(-1)

    parents = tree_parent.reshape(-1, 1)
    half = LANES // 2
    angles = jnp.exp(-THETA_LOG * 2.0 * jnp.arange(half, dtype=F32) / LANES)
    angles = jnp.concatenate([angles, angles])[None, :]
    gain = norm_gain.reshape(-1, hidden.shape[1])
    info = jnp.full((1,), spot, I32)
    far_mine = lax.dynamic_index_in_dim(far_len, me, 0, keepdims=False)
    far_other = lax.dynamic_index_in_dim(far_len, me ^ 1, 0, keepdims=False)

    weights = (q_weight, k_weight, v_weight)
    longs = pair_slot.shape[1]
    scalars = (info, order, rank, cache_len, pair_slot, far_mine, accept_node)
    tables_in = (parents, angles, gain)
    *state, picked0, long_queries = project_first(
        places[0],
        tree,
        longs,
        scalars,
        tables_in,
        weights,
        (hidden, hidden_core, from_x[0], from_xc[0]),
    )
    far_queries = swap(long_queries, "grp", 1)
    out, long_acc, long_sum, far_done = attend_first(
        places[0],
        tree,
        longs,
        requests,
        scalars[1:5],
        far_other,
        tables,
        state,
        far_queries,
        pool,
        moved,
        page_size,
        token_rows,
    )
    back = swap(far_done, "grp", 1)
    out, picked1 = finish(
        places[1],
        tree,
        longs,
        requests,
        scalars,
        tables_in,
        weights,
        (hidden, hidden_core, from_x[1], from_xc[1]),
        tables,
        pool,
        moved,
        page_size,
        out,
    )
    out, accepted = merge(
        tree, pair_slot, rank, long_acc, long_sum, back, (picked0, picked1), out
    )
    return (out, accepted)


def chunk_counts(requests):
    return (requests // 4, requests - requests // 4)


def solution(mesh):
    in_specs = (
        P("grp", "tp"),
        P(),
        P(None, "tp"),
        P(None, "tp"),
        P(None, "tp"),
        P("grp", None, "tp", None),
        P("grp", None),
        P("grp"),
        P("grp", None),
        P("grp"),
        P("grp", None),
        P(),
        P("grp", None),
        P("grp"),
        P("grp"),
    )
    out_specs = (P("grp", "tp"), P("grp", "tp", None))
    chosen = body if mesh.shape["tp"] == 4 else general_body
    return jax.shard_map(chosen, mesh=mesh, in_specs=in_specs, out_specs=out_specs, check_vma=False)
```

```python
import jax
import jax.numpy as jnp
from jax import lax
from jax.experimental import pallas as pl
from jax.experimental.pallas import tpu as pltpu
from jax.sharding import PartitionSpec as P

D = 4608
CAP = 4
ACCEPT = 5


THETA_LOG = 9.210340371976184
SCORE_SCALE = 144.0 ** (-0.5)
LOGIT_CAP = 50.0
HIGHEST = lax.Precision.HIGHEST
IN_SCALE = SCORE_SCALE / LOGIT_CAP
OUT_SCALE = LOGIT_CAP * 1.4426950408889634
LANES = 128
BLOCK = 256
GROUPED = 6
PAIR = 4
MIB = 2**20
ANY = pl.BlockSpec(memory_space=pl.ANY)
VMEM = pl.BlockSpec(memory_space=pltpu.VMEM)
SMEM = pl.BlockSpec(memory_space=pltpu.SMEM)
BF16 = jnp.bfloat16
F32 = jnp.float32
I32 = jnp.int32


def estimate(micros):
    return pl.CostEstimate(flops=int(micros * 1.15e9), bytes_accessed=0, transcendentals=0)


def params(mib):
    return pltpu.CompilerParams(vmem_limit_bytes=mib * MIB)


def shape(dims, dtype):
    return jax.ShapeDtypeStruct(dims, dtype)


def aligned(index, unit):
    return pl.multiple_of(index * unit, unit)


def partner(value, axis, bit):
    mask = 2**bit
    pairs = [(source, source ^ mask) for source in range(lax.axis_size(axis))]
    return lax.ppermute(value, axis, pairs)


def rotate(values, position):
    halfway = values.shape[-1] // 2
    angles = jnp.exp(-THETA_LOG * 2.0 * jnp.arange(halfway, dtype=jnp.float32) / values.shape[-1])
    phases = position.astype(jnp.float32)[:, None] * angles[None, :]
    cosine = jnp.cos(phases)[:, None, :]
    sine_part = jnp.sin(phases)[:, None, :]
    former = values[..., :halfway]
    latter = values[..., halfway:]
    return jnp.concatenate(
        [former * cosine - latter * sine_part, latter * cosine + former * sine_part], -1
    )


def ancestry(parents):
    length = parents.shape[-1]
    labels = jnp.arange(length, dtype=jnp.int32)
    reached = (parents[..., :, None] == labels).astype(jnp.float32) + jnp.eye(
        length, dtype=jnp.float32
    )
    reached = jnp.minimum(jnp.einsum("nij,njk->nik", reached, reached, precision=HIGHEST), 1.0)
    reached = jnp.minimum(jnp.einsum("nij,njk->nik", reached, reached, precision=HIGHEST), 1.0)
    depths = jnp.sum((reached > 0.5).astype(jnp.int32), -1) - 1
    return (reached, depths)


def absorb(running, queries, keys_block, values_block, allowed):
    largest, summed, weighted = running
    scores = (
        jnp.einsum("igrd,tgd->igrt", queries, keys_block, preferred_element_type=jnp.float32)
        * SCORE_SCALE
    )
    scores = LOGIT_CAP * jnp.tanh(scores / LOGIT_CAP)
    weights = jnp.where(allowed, jnp.exp(scores - LOGIT_CAP), 0.0)
    summed = summed + jnp.sum(weights, -1)
    weighted = weighted + jnp.einsum(
        "igrt,tgd->igrd",
        weights.astype(jnp.bfloat16),
        values_block,
        preferred_element_type=jnp.float32,
    )
    return (largest, summed, weighted)


def empty_state(queries):
    leading = queries.shape[:3]
    return (
        jnp.full(leading, LOGIT_CAP, jnp.float32),
        jnp.zeros(leading, jnp.float32),
        jnp.zeros(queries.shape, jnp.float32),
    )


def attend_blocks(queries, loader, length, block_span):
    turns = (length + block_span - 1) // block_span

    def advance(number, running):
        keys_block, values_block = loader(number)
        allowed = (number * block_span + jnp.arange(block_span, dtype=jnp.int32) < length)[
            None, None, None, :
        ]
        return absorb(running, queries, keys_block, values_block, allowed)

    return lax.fori_loop(0, turns, advance, empty_state(queries))


def combine(states):
    summed = jnp.zeros(states[0][1].shape, jnp.float32)
    weighted = jnp.zeros(states[0][2].shape, jnp.float32)
    for state in states:
        summed = summed + state[1]
        weighted = weighted + state[2]
    return weighted / summed[..., None]


def general_body(
    hidden,
    norm_gain,
    q_weight,
    k_weight,
    v_weight,
    kv_pages,
    page_table,
    cache_len,
    tree_parent,
    accept_node,
    pair_slot,
    far_len,
    far_table,
    mig_src,
    mig_page,
):
    token_rows = hidden.shape[0]
    requests = cache_len.shape[0]
    tree_size = tree_parent.shape[1]
    head_size = kv_pages.shape[3] // 2
    local_heads = kv_pages.shape[2]
    page_size = kv_pages.shape[1]
    table_width = page_table.shape[1]
    long_count = pair_slot.shape[1]
    migrations = mig_src.shape[0]
    groups = lax.axis_size("grp")
    myself = lax.axis_index("grp")
    widened = lax.all_gather(hidden, "tp", axis=1, tiled=True).astype(jnp.float32)
    scaled = (widened * norm_gain[None, :]).astype(jnp.bfloat16)
    query_sum = jnp.dot(scaled, q_weight, preferred_element_type=jnp.float32)
    key_sum = jnp.dot(scaled, k_weight, preferred_element_type=jnp.float32)
    value_sum = jnp.dot(scaled, v_weight, preferred_element_type=jnp.float32)
    squares = jnp.sum(widened * widened, 1)
    query_sum, key_sum, value_sum, squares = (query_sum, key_sum, value_sum, squares)
    row_scale = lax.rsqrt(squares / D + 1e-06)[:, None]
    reached, depths = ancestry(tree_parent)
    far_mine = lax.dynamic_index_in_dim(far_len, myself, 0, keepdims=False)
    long_slots = pair_slot[0]
    matched = jnp.arange(requests, dtype=jnp.int32)[:, None] == long_slots[None, :]
    far_own = jnp.sum(jnp.where(matched, far_mine[None, :], 0), 1)
    position = ((cache_len + far_own)[:, None] + depths).reshape(-1)
    queries = rotate(
        (query_sum * row_scale).reshape(token_rows, 2 * local_heads, head_size), position
    ).astype(jnp.bfloat16)
    keys_new = rotate(
        (key_sum * row_scale).reshape(token_rows, local_heads, head_size), position
    ).astype(jnp.bfloat16)
    values_new = (
        (value_sum * row_scale).astype(jnp.bfloat16).reshape(token_rows, local_heads, head_size)
    )
    order_index = jnp.arange(migrations, dtype=jnp.int32)
    earlier = order_index[:, None] > order_index[None, :]

    def rank_of(sources):
        return jnp.sum(
            ((sources[..., :, None] == sources[..., None, :]) & earlier).astype(jnp.int32), -1
        )

    own_rank = rank_of(mig_src)
    slot_index = jnp.arange(CAP, dtype=jnp.int32)
    every_source, every_page = (
        lax.all_gather(mig_src, "grp", axis=0, tiled=True),
        lax.all_gather(mig_page, "grp", axis=0, tiled=True),
    )
    every_source = every_source.reshape(groups, migrations)
    every_page = every_page.reshape(groups, migrations)
    every_rank = rank_of(every_source)
    hits = (every_source[:, :, None] == myself) & (
        every_rank[:, :, None] == slot_index[None, None, :]
    )
    wanted = jnp.sum(jnp.where(hits, every_page[:, :, None] + 1, 0), 1) - 1
    present = (wanted >= 0)[:, :, None, None, None]
    outgoing = jnp.where(present, kv_pages[jnp.maximum(wanted, 0)], jnp.zeros((), jnp.bfloat16))
    incoming = lax.all_to_all(outgoing, "grp", split_axis=0, concat_axis=0, tiled=True)
    moved = incoming.reshape(groups * CAP, page_size, local_heads, 2 * head_size)[
        mig_src * CAP + own_rank
    ]
    extended = jnp.concatenate([kv_pages, moved], 0)
    block_pages = min(32, table_width)
    block_span = block_pages * page_size

    def page_loader(table_row):

        def loader(number):
            chosen = lax.dynamic_slice_in_dim(table_row, number * block_pages, block_pages, 0)
            gathered = extended[chosen].reshape(block_span, local_heads, 2 * head_size)
            return (gathered[..., :head_size], gathered[..., head_size:])

        return loader

    grouped = queries.reshape(requests, tree_size, local_heads, 2, head_size)
    long_queries = grouped[long_slots]
    far_dense = extended[far_table].reshape(
        long_count, table_width * page_size, local_heads, 2 * head_size
    )
    arrived = partner(far_dense, "grp", 0)

    def owner_part(packed):
        query_block, cache_block, length = packed

        def loader(number):
            portion = lax.dynamic_slice_in_dim(cache_block, number * block_span, block_span, 0)
            return (portion[..., :head_size], portion[..., head_size:])

        return attend_blocks(query_block, loader, length, block_span)

    far_parts = lax.map(owner_part, (long_queries, arrived, far_mine))
    keys_grouped = keys_new.reshape(requests, tree_size, local_heads, head_size)
    values_grouped = values_new.reshape(requests, tree_size, local_heads, head_size)

    def request_part(packed):
        query_block, key_block, value_block, table_row, length, tree_mask, match_row = packed
        own_state = attend_blocks(query_block, page_loader(table_row), length, block_span)
        tree_state = absorb(
            empty_state(query_block),
            query_block,
            key_block,
            value_block,
            (tree_mask > 0.5)[:, None, None, :],
        )
        chooser = match_row[:, None, None, None]
        far_state = (
            own_state[0],
            jnp.sum(jnp.where(chooser, far_parts[1], 0.0), 0),
            jnp.sum(jnp.where(match_row[:, None, None, None, None], far_parts[2], 0.0), 0),
        )
        mixed = combine((own_state, tree_state, far_state))
        return mixed.reshape(tree_size, 2 * local_heads * head_size).astype(jnp.bfloat16)

    attn_out = lax.map(
        request_part,
        (grouped, keys_grouped, values_grouped, page_table, cache_len, reached, matched),
    ).reshape(token_rows, 2 * local_heads * head_size)
    leaves = (jnp.arange(tree_size, dtype=jnp.int32)[None, :] == accept_node[:, None]).astype(
        jnp.float32
    )
    lineage = jnp.einsum("rt,rtj->rj", leaves, reached, precision=HIGHEST)
    levels = (depths[:, None, :] == jnp.arange(ACCEPT, dtype=jnp.int32)[None, :, None]).astype(
        jnp.float32
    )
    picker = lineage[:, None, :] * levels
    fresh_rows = (
        jnp.concatenate([keys_new, values_new], -1)
        .reshape(requests, tree_size, local_heads * 2 * head_size)
        .astype(jnp.float32)
    )
    accepted = (
        jnp.einsum("rpt,rtc->rpc", picker, fresh_rows, precision=HIGHEST)
        .astype(jnp.bfloat16)
        .reshape(requests * ACCEPT, local_heads, 2 * head_size)
    )
    return (attn_out, accepted)


def order_rows(hidden, pair_slot, cache_len, mig_src, mig_page, own_pages, groups, tree_size, counts):
    requests, longs = cache_len.shape[0], pair_slot.shape[1]
    migrations = mig_src.shape[0]
    width = hidden.shape[1]

    def kernel(
        pair_ref, length_ref, source_ref, page_ref, hidden_ref, order_ref, rank_ref, asked, placed, *outs
    ):
        taken = [jnp.int32(0)] * migrations
        for i in range(migrations):
            for j in range(i):
                taken[i] = taken[i] + (source_ref[i] == source_ref[j]).astype(I32)
        for i in range(groups):
            for j in range(CAP):
                asked[i, j] = jnp.int32(0)
        for i in range(migrations):
            asked[source_ref[i], taken[i]] = page_ref[i]
            placed[i] = own_pages + source_ref[i] * CAP + taken[i]
        weight = []
        for i in range(requests):
            value = length_ref[i]
            for j in range(longs):
                value = value + jnp.where(pair_ref[0, j] == i, 1 << 20, 0)
            weight.append(value)
        ranks = [jnp.int32(0)] * requests
        for i in range(requests):
            for j in range(i):
                ahead = (weight[j] >= weight[i]).astype(I32)
                ranks[i] = ranks[i] + ahead
                ranks[j] = ranks[j] + 1 - ahead
        for i in range(requests):
            order_ref[ranks[i]] = jnp.int32(i)
            rank_ref[i] = ranks[i]
        place = 0
        for out, count in zip(outs, counts, strict=True):
            for i in range(count):
                out[pl.ds(i * tree_size, tree_size), :] = hidden_ref[
                    pl.ds(aligned(order_ref[place], tree_size), tree_size), :
                ]
                place += 1

    return pl.pallas_call(
        kernel,
        out_shape=[
            *[shape((requests,), I32)] * 2,
            shape((groups, CAP), I32),
            shape((migrations,), I32),
            *[shape((count * tree_size, width), BF16) for count in counts],
        ],
        in_specs=[SMEM] * 4 + [VMEM],
        out_specs=[SMEM] * 4 + [VMEM] * len(counts),
        cost_estimate=estimate(2),
        compiler_params=params(8),
        name="order_rows",
    )(*[hbm(a) for a in (pair_slot, cache_len, mig_src, mig_page)], hidden)


def pick_pages(pages, wanted):
    peers, slots = wanted.shape

    def kernel(wanted_ref, pages_ref, out, sem):
        copies = []
        for peer in range(peers):
            for slot in range(slots):
                copies.append(
                    pltpu.make_async_copy(
                        pages_ref.at[wanted_ref[peer, slot]],
                        out.at[peer, slot],
                        sem.at[peer * slots + slot],
                    )
                )
                copies[-1].start()
        for copy in copies:
            copy.wait()

    return pl.pallas_call(
        kernel,
        out_shape=shape((peers, slots, *pages.shape[1:]), BF16),
        in_specs=[SMEM, ANY],
        out_specs=VMEM,
        scratch_shapes=[pltpu.SemaphoreType.DMA((peers * slots,))],
        cost_estimate=estimate(1.5),
        compiler_params=params(4),
        name="pick_pages",
    )(wanted, hbm(pages))


def project_core(places, tree, longs, depth_all, info, inputs, scratch, q_ref, acc_ref, sum_ref, picked_out, long_out, started=lambda: None):
    (info_ref, order_ref, rank_ref, length_ref, pair_ref, far_ref, accept_ref) = info
    (parents_ref, angles_ref, gain_ref, *weight_refs, own_ref, core_ref, x_ref, xc_ref) = inputs
    (blocks, reached_ref, *kept, q_sum, k_sum, v_sum, square_sum, sem, weight_sem) = scratch
    totals = (q_sum, k_sum, v_sum)
    count = len(places)
    paired = PAIR * tree
    padded = -(-paired // LANES) * LANES
    filler = padded - paired
    quarter = blocks.shape[2]
    heads = kept[0].shape[1] // LANES
    kv_heads = kept[1].shape[1] // LANES
    share = heads // kv_heads
    per_item = heads * tree
    requests = [order_ref[place] for place in places]
    me = info_ref[0]
    loads = []
    for part in range(4):
        span = pl.ds(aligned(me ^ part, quarter), quarter)
        if part < 2:
            source = (own_ref, core_ref)[part]
            for i, request in enumerate(requests):
                loads.append(
                    pltpu.make_async_copy(
                        source.at[pl.ds(aligned(request, tree), tree)],
                        blocks.at[part, pl.ds(i * tree, tree)],
                        sem.at[part],
                    )
                )
        else:
            source = (x_ref, xc_ref)[part - 2]
            loads.append(pltpu.make_async_copy(source, blocks.at[part], sem.at[part]))
        for number, (source, target) in enumerate(zip(weight_refs, kept, strict=True)):
            loads.append(
                pltpu.make_async_copy(
                    source.at[span], target.at[span], weight_sem.at[part, number]
                )
            )
    for load in loads:
        load.start()
    started()
    labels = lax.broadcasted_iota(I32, (padded, padded), 1)
    mine = lax.broadcasted_iota(I32, (padded, padded), 0)
    reached, depth_columns, depth_rows = [], [], []
    for p in range(count // PAIR):
        column = []
        for i in range(PAIR):
            part = parents_ref[pl.ds(aligned(requests[p * PAIR + i], tree), tree), :]
            column.append(jnp.where(part < 0, -1, part + i * tree))
        column = jnp.concatenate([*column, jnp.full((filler, 1), -1, I32)], 0)
        step = ((column == labels) | (mine == labels)).astype(F32).astype(BF16)
        step = jnp.minimum(jnp.dot(step, step, preferred_element_type=F32), 1.0).astype(BF16)
        whole = jnp.minimum(jnp.dot(step, step, preferred_element_type=F32), 1.0)
        reached_ref[p * padded : (p + 1) * padded, :] = whole
        reached.append(whole[:paired])
        depth_columns.append(jnp.sum(whole[:paired], 1, keepdims=True) - 1.0)
        depth_rows.append(
            lax.dot_general(
                jnp.ones((16, padded), BF16),
                whole.astype(BF16),
                (((1,), (1,)), ((), ())),
                preferred_element_type=F32,
            )
            - 1.0
        )
    bases = []
    for request in requests:
        base = length_ref[request]
        for j in range(longs):
            base = base + jnp.where(pair_ref[0, j] == request, far_ref[j], 0)
        bases.append(jnp.full((tree, 1), base, I32))
    position = jnp.concatenate(bases, 0).astype(F32) + jnp.concatenate(depth_columns, 0)
    phases = position * angles_ref[...]
    cosine = jnp.cos(phases)
    half = LANES // 2
    sign = jnp.where(lax.broadcasted_iota(I32, (1, LANES), 1) < half, -1.0, 1.0)
    sine = jnp.sin(phases) * sign
    square_sum[...] = jnp.zeros_like(square_sum)
    for total in totals:
        total[...] = jnp.zeros_like(total)

    def part_step(part, carried):
        which = me ^ part
        span = pl.ds(aligned(which, quarter), quarter)
        pltpu.make_async_copy(x_ref, blocks.at[part], sem.at[part]).wait()
        for number, (source, target) in enumerate(zip(weight_refs, kept, strict=True)):
            pltpu.make_async_copy(
                source.at[span], target.at[span], weight_sem.at[part, number]
            ).wait()
        wide = blocks[part].astype(F32)
        square = wide * wide
        folded = square[:, :LANES]
        for c in range(1, quarter // LANES):
            folded = folded + square[:, c * LANES : (c + 1) * LANES]
        square_sum[...] += folded
        scaled = (wide * gain_ref[pl.ds(which, 1), :]).astype(BF16)
        for ref, total in zip(kept, totals, strict=True):
            total[...] += jnp.dot(scaled, ref[span, :], preferred_element_type=F32)
        return carried

    lax.fori_loop(0, 4, part_step, 0)
    sums = [total[...] for total in totals]
    squares = jnp.sum(square_sum[...], 1, keepdims=True)
    row_scale = lax.rsqrt(squares / depth_all + 1e-06)

    def rope(values):
        return (values * cosine + pltpu.roll(values, half, 1) * sine).astype(BF16)

    def head_of(values, h):
        return values[:, h * LANES : (h + 1) * LANES] * row_scale

    keys = [rope(head_of(sums[1], g)) for g in range(kv_heads)]
    values = [head_of(sums[2], g).astype(BF16) for g in range(kv_heads)]

    def pad(block):
        return jnp.concatenate([block, jnp.zeros((filler, LANES), BF16)], 0)

    queries = [rope(head_of(sums[0], h)) for h in range(heads)]
    zeros = jnp.zeros((tree, LANES), BF16)
    levels = lax.broadcasted_iota(I32, (16, padded), 0).astype(F32)
    pairs = range(count // PAIR)
    cuts = [slice(p * paired, (p + 1) * paired) for p in pairs]
    pair_keys = [[pad(block[cut]) for block in keys] for cut in cuts]
    pair_values = [[pad(block[cut]) for block in values] for cut in cuts]
    each = [(p, g) for p in pairs for g in range(kv_heads)]
    scores = [
        lax.dot_general(
            jnp.concatenate([queries[g * share + r][cuts[p]] for r in range(share)], 0),
            pair_keys[p][g],
            (((1,), (1,)), ((), ())),
            preferred_element_type=F32,
        )
        for p, g in each
    ]
    masks = [jnp.concatenate([block] * share, 0) for block in reached]
    exped = [
        jnp.exp2(jnp.tanh(score * IN_SCALE) * OUT_SCALE) * masks[p]
        for (p, g), score in zip(each, scores, strict=True)
    ]
    mixed = [
        jnp.dot(block.astype(BF16), pair_values[p][g], preferred_element_type=F32)
        for (p, g), block in zip(each, exped, strict=True)
    ]
    pickers = []
    for p in pairs:
        picks = []
        for i in range(PAIR):
            leaf = accept_ref[requests[p * PAIR + i]] + p * padded + i * tree
            picks.append(jnp.where(depth_rows[p] == levels, reached_ref[pl.ds(leaf, 1), :], 0.0))
        pickers.append(jnp.concatenate(picks, 0).astype(BF16))
    picked = []
    for p in pairs:
        fresh = [block for g in range(kv_heads) for block in (pair_keys[p][g], pair_values[p][g])]
        picked.append(
            jnp.dot(pickers[p], jnp.concatenate(fresh, 1), preferred_element_type=F32)
        )
    for (p, g), block, weight in zip(each, mixed, exped, strict=True):
        total = weight[:, :LANES]
        for c in range(1, padded // LANES):
            total = total + weight[:, c * LANES : (c + 1) * LANES]
        for r in range(share):
            h = g * share + r
            for i in range(PAIR):
                start = (p * PAIR + i) * per_item + h * tree
                there = slice(start, start + tree)
                inside = slice(r * paired + i * tree, r * paired + (i + 1) * tree)
                acc_ref[there, :] = block[inside]
                sum_ref[there, :] = total[inside]
                first = p * paired + i * tree
                for other in range(kv_heads):
                    q_ref[there, other * LANES : (other + 1) * LANES] = (
                        queries[h][first : first + tree] if other == g else zeros
                    )
    for p in pairs:
        picked_out[p * PAIR * 16 : (p + 1) * PAIR * 16, :] = picked[p].astype(BF16)
    if long_out is not None:
        for j in range(longs):
            place = rank_ref[pair_ref[0, j]]
            long_out[j * per_item : (j + 1) * per_item, :] = q_ref[
                pl.ds(aligned(place, per_item), per_item), :
            ]


def project_scratch(count, tree, hidden, weights):
    padded = -(-PAIR * tree // LANES) * LANES
    return [
        pltpu.VMEM((4, count * tree, hidden.shape[1]), BF16),
        pltpu.VMEM((count // PAIR * padded, padded), F32),
        *[pltpu.VMEM(weight.shape, BF16) for weight in weights],
        *[pltpu.VMEM((count * tree, weight.shape[1]), F32) for weight in weights],
        pltpu.VMEM((count * tree, LANES), F32),
        pltpu.SemaphoreType.DMA((4,)),
        pltpu.SemaphoreType.DMA((4, len(weights))),
    ]


def state_scratch(count, per_item, width):
    return [
        pltpu.VMEM((count * per_item, width), BF16),
        pltpu.VMEM((count * per_item, LANES), F32),
        pltpu.VMEM((count * per_item, LANES), F32),
    ]


def hbm(array):
    return pltpu.with_memory_space_constraint(array, pltpu.HBM)


def project_first(places, tree, longs, scalars, tables, weights, parts):
    count = len(places)
    hidden = parts[0]
    heads = weights[0].shape[1] // LANES
    width = weights[1].shape[1]
    per_item = heads * tree
    depth_all = weights[0].shape[0]
    n_scratch = len(project_scratch(count, tree, hidden, weights))

    def kernel(*refs):
        info, refs = refs[:7], refs[7:]
        inputs, refs = refs[:10], refs[10:]
        outs, (picked_out, long_out), refs = refs[:3], refs[3:5], refs[5:]
        state, scratch, sem = refs[:3], refs[3 : 3 + n_scratch], refs[-1]
        project_core(
            places, tree, longs, depth_all, info, inputs, scratch, *state, picked_out, long_out
        )
        copies = [
            pltpu.make_async_copy(source, target, sem.at[i])
            for i, (source, target) in enumerate(zip(state, outs, strict=True))
        ]
        for copy in copies:
            copy.start()
        for copy in copies:
            copy.wait()

    rows = count * per_item
    return pl.pallas_call(
        kernel,
        out_shape=[
            pltpu.HBM((rows, width), BF16),
            pltpu.HBM((rows, LANES), F32),
            pltpu.HBM((rows, LANES), F32),
            shape((count * 16, 2 * width), BF16),
            shape((longs * per_item, width), BF16),
        ],
        in_specs=[SMEM] * 7 + [VMEM] * 3 + [ANY] * 7,
        out_specs=[ANY] * 3 + [VMEM] * 2,
        scratch_shapes=[
            *state_scratch(count, per_item, width),
            *project_scratch(count, tree, hidden, weights),
            pltpu.SemaphoreType.DMA((3,)),
        ],
        compiler_params=params(40),
        cost_estimate=estimate(1),
        name="project_first",
    )(*scalars, *tables, *[hbm(a) for a in (*weights, *parts[:2])], *parts[2:])


def attend_core(lens, rows_of, table_ref, cache, qs, acc, sums, score_refs, weight_refs, page_size):
    count = lens.shape[0]
    width = qs.shape[1]
    kv_heads = width // LANES
    per_item = qs.shape[0] // count
    half = per_item // kv_heads
    pages = BLOCK // page_size
    blocks = jnp.int32(0)
    for i in range(count):
        blocks = blocks + (lens[i] + BLOCK - 1) // BLOCK
    def following(state):
        item, block = state
        last = (block + 1) * BLOCK >= lens[item]
        return (
            jnp.where(last, jnp.minimum(item + 1, count - 1), item),
            jnp.where(last, 0, block + 1),
        )

    def gathered(state, first):
        item, block = state
        base = rows_of[item] + block * pages
        spans = [
            pl.ds(aligned(table_ref[base + j], page_size), page_size) for j in range(pages)
        ]
        sides = []
        for g in range(kv_heads):
            lanes = slice((2 * g + first) * LANES, (2 * g + first + 1) * LANES)
            sides.append(jnp.concatenate([cache[span, lanes] for span in spans], 0))
        return jnp.concatenate(sides, 1)

    def score(state, scores):
        item = state[0]
        scores[...] = lax.dot_general(
            qs[pl.ds(aligned(item, per_item), per_item), :],
            gathered(state, 0),
            (((1,), (1,)), ((), ())),
            preferred_element_type=F32,
        )

    def weigh(state, number, scores, weights):
        item, block = state
        left = jnp.where(number < blocks, lens[item] - block * BLOCK, 0)
        allowed = lax.broadcasted_iota(I32, (1, BLOCK), 1) < left
        exped = jnp.exp2(jnp.tanh(scores[...] * IN_SCALE) * OUT_SCALE)
        exped = jnp.where(allowed, exped, 0.0)
        weights[...] = exped.astype(BF16)
        part = exped[:, :LANES]
        for c in range(1, BLOCK // LANES):
            part = part + exped[:, c * LANES : (c + 1) * LANES]
        sums[pl.ds(aligned(item, per_item), per_item), :] += part

    def mix(state, weights):
        item = state[0]
        mixed = jnp.dot(
            weights[...], gathered(state, 1), preferred_element_type=F32
        )
        for g in range(kv_heads):
            there = pl.ds(aligned(item * kv_heads + g, half), half)
            acc[there, :] += mixed[
                g * half : (g + 1) * half, g * LANES : (g + 1) * LANES
            ]

    def group_from(state):
        states = [state]
        for _ in range(GROUPED - 1):
            states.append(following(states[-1]))
        return states, following(states[-1])

    group0, next0 = group_from((jnp.int32(0), jnp.int32(0)))
    for u in range(GROUPED):
        score(group0[u], score_refs[u])
    for u in range(GROUPED):
        weigh(group0[u], u, score_refs[u], weight_refs[u])
    group1, next1 = group_from(next0)
    for u in range(GROUPED):
        score(group1[u], score_refs[u])

    def turn(number, carried):
        state0, state1, state2 = carried
        now0, _ = group_from(state0)
        now1, _ = group_from(state1)
        now2, state3 = group_from(state2)
        for u in range(GROUPED):
            mix(now0[u], weight_refs[u])
            weigh(now1[u], (number + 1) * GROUPED + u, score_refs[u], weight_refs[u])
            score(now2[u], score_refs[u])
        return state1, state2, state3

    lax.fori_loop(
        0,
        (blocks + GROUPED - 1) // GROUPED,
        turn,
        ((jnp.int32(0), jnp.int32(0)), next0, next1),
    )


def attend_scratch(count, per_item, cache_rows, cache_width):
    return [
        pltpu.VMEM((cache_rows, cache_width), BF16),
        pltpu.SMEM((count,), I32),
        pltpu.SMEM((count,), I32),
        *[pltpu.VMEM((per_item, BLOCK), F32) for _ in range(GROUPED)],
        *[pltpu.VMEM((per_item, BLOCK), BF16) for _ in range(GROUPED)],
    ]


def lay(target, block, tree):
    for h in range(block.shape[0] // tree):
        target[:, h * LANES : (h + 1) * LANES] = block[h * tree : (h + 1) * tree].astype(
            BF16
        )


def bring_cache(pool_ref, moved_ref, cache, sem):
    rows = pool_ref.shape[0]
    quarter = rows // 4
    copies = [
        pltpu.make_async_copy(
            pool_ref.at[pl.ds(c * quarter, quarter)],
            cache.at[pl.ds(c * quarter, quarter)],
            sem.at[c],
        )
        for c in range(4)
    ]
    copies.append(
        pltpu.make_async_copy(moved_ref, cache.at[pl.ds(rows, moved_ref.shape[0])], sem.at[4])
    )
    for copy in copies:
        copy.start()
    return copies


def send_out(number, request, staged, out_ref, sem, tree):
    copy = pltpu.make_async_copy(
        staged.at[number], out_ref.at[pl.ds(aligned(request, tree), tree)], sem.at[number]
    )
    copy.start()
    return copy


def attend_first(
    places, tree, longs, requests, scalars, far_len, table, state, far_queries, pool, moved, page_size, token_rows
):
    own = len(places)
    count = own + longs
    rows, width = state[0].shape
    per_item = rows // own
    heads = per_item // tree
    far_rows = longs * per_item
    table_width = table.shape[0] // (requests + longs)
    cache_rows, cache_width = pool.shape[0] + moved.shape[0], pool.shape[1]

    def kernel(*refs):
        (order_ref, rank_ref, length_ref, pair_ref, far_ref, table_ref), refs = refs[:6], refs[6:]
        state_refs, (far_q, pool_ref, moved_ref), refs = refs[:3], refs[3:6], refs[6:]
        (out_ref, long_acc, long_sum, far_out), refs = refs[:4], refs[4:]
        (qs, acc, sums), (staged, sem, cache_sem), refs = refs[:3], refs[3:6], refs[6:]
        (cache, lens, rows_of), refs = refs[:3], refs[3:]
        copies = bring_cache(pool_ref, moved_ref, cache, cache_sem)
        for i, (source, target) in enumerate(zip(state_refs, (qs, acc, sums), strict=True)):
            copies.append(pltpu.make_async_copy(source, target.at[pl.ds(0, rows)], sem.at[i]))
            copies[-1].start()
        copies.append(pltpu.make_async_copy(far_q, qs.at[pl.ds(rows, far_rows)], sem.at[3]))
        copies[-1].start()
        acc[rows:, :] = jnp.zeros((far_rows, LANES), F32)
        sums[rows:, :] = jnp.zeros((far_rows, LANES), F32)
        for i, place in enumerate(places):
            request = order_ref[place]
            lens[i] = length_ref[request]
            rows_of[i] = request * table_width
        for j in range(longs):
            lens[own + j] = far_ref[j]
            rows_of[own + j] = (requests + j) * table_width
        for copy in copies:
            copy.wait()
        attend_core(
            lens, rows_of, table_ref, cache, qs, acc, sums, refs[:GROUPED], refs[GROUPED:], page_size
        )
        total = jnp.sum(sums[rows:, :], 1, keepdims=True)
        far_out[:, :LANES] = acc[rows:, :].astype(BF16)
        far_out[:, LANES:] = jnp.broadcast_to(total, (far_rows, LANES)).astype(BF16)
        sent = []
        for i, place in enumerate(places):
            there = slice(i * per_item, (i + 1) * per_item)
            lay(staged.at[i], acc[there, :] / jnp.sum(sums[there, :], 1, keepdims=True), tree)
            sent.append(send_out(i, order_ref[place], staged, out_ref, sem, tree))
        for j in range(longs):
            there = slice(j * per_item, (j + 1) * per_item)
            here = pl.ds(aligned(rank_ref[pair_ref[0, j]], per_item), per_item)
            long_acc[there, :] = acc[here, :]
            long_sum[there, :] = sums[here, :]
        for copy in sent:
            copy.wait()

    return pl.pallas_call(
        kernel,
        out_shape=[
            pltpu.HBM((token_rows, heads * LANES), BF16),
            shape((far_rows, LANES), F32),
            shape((far_rows, LANES), F32),
            shape((far_rows, 2 * LANES), BF16),
        ],
        in_specs=[SMEM] * 6 + [ANY] * 6,
        out_specs=[ANY] + [VMEM] * 3,
        scratch_shapes=[
            *state_scratch(count, per_item, width),
            pltpu.VMEM((own, tree, heads * LANES), BF16),
            pltpu.SemaphoreType.DMA((max(own, 4),)),
            pltpu.SemaphoreType.DMA((5,)),
            *attend_scratch(count, per_item, cache_rows, cache_width),
        ],
        compiler_params=params(32),
        cost_estimate=estimate(18),
        name="attend_first",
    )(*scalars, far_len, table, *[hbm(a) for a in state], far_queries, hbm(pool), hbm(moved))


def finish(
    places, tree, longs, requests, scalars, tables, weights, parts, table, pool, moved, page_size, out
):
    own = len(places)
    hidden = parts[0]
    heads = weights[0].shape[1] // LANES
    width = weights[1].shape[1]
    per_item = heads * tree
    depth_all = weights[0].shape[0]
    n_scratch = len(project_scratch(own, tree, hidden, weights))
    table_width = table.shape[0] // (requests + longs)
    cache_rows, cache_width = pool.shape[0] + moved.shape[0], pool.shape[1]

    def kernel(*refs):
        info, table_ref, refs = refs[:7], refs[7], refs[8:]
        order_ref, length_ref = info[1], info[3]
        inputs, refs = refs[:10], refs[10:]
        (pool_ref, moved_ref), refs = refs[:2], refs[3:]
        (out_ref, picked_out), refs = refs[:2], refs[2:]
        (qs, acc, sums), (staged, sem, cache_sem), refs = refs[:3], refs[3:6], refs[6:]
        scratch, refs = refs[:n_scratch], refs[n_scratch:]
        (cache, lens, rows_of), refs = refs[:3], refs[3:]
        for i, place in enumerate(places):
            request = order_ref[place]
            lens[i] = length_ref[request]
            rows_of[i] = request * table_width
        copies = []
        project_core(
            places, tree, longs, depth_all, info, inputs, scratch, qs, acc, sums, picked_out, None,
            lambda: copies.extend(bring_cache(pool_ref, moved_ref, cache, cache_sem)),
        )

        @pl.when(info[0][0] >= 0)
        def _():
            for copy in copies:
                copy.wait()

        attend_core(
            lens, rows_of, table_ref, cache, qs, acc, sums, refs[:GROUPED], refs[GROUPED:], page_size
        )
        sent = []
        for i, place in enumerate(places):
            there = slice(i * per_item, (i + 1) * per_item)
            lay(staged.at[i], acc[there, :] / jnp.sum(sums[there, :], 1, keepdims=True), tree)
            sent.append(send_out(i, order_ref[place], staged, out_ref, sem, tree))
        for copy in sent:
            copy.wait()

    operands = [*scalars, table, *tables]
    operands += [hbm(a) for a in (*weights, *parts[:2])]
    operands += [*parts[2:], *[hbm(a) for a in (pool, moved, out)]]
    return pl.pallas_call(
        kernel,
        out_shape=[pltpu.HBM(out.shape, BF16), shape((own * 16, 2 * width), BF16)],
        in_specs=[SMEM] * 8 + [VMEM] * 3 + [ANY] * 10,
        out_specs=[ANY, VMEM],
        scratch_shapes=[
            *state_scratch(own, per_item, width),
            pltpu.VMEM((own, tree, heads * LANES), BF16),
            pltpu.SemaphoreType.DMA((own,)),
            pltpu.SemaphoreType.DMA((5,)),
            *project_scratch(own, tree, hidden, weights),
            *attend_scratch(own, per_item, cache_rows, cache_width),
        ],
        input_output_aliases={len(operands) - 1: 0},
        compiler_params=params(48),
        cost_estimate=estimate(18),
        name="finish",
    )(*operands)


def merge(tree, pair_slot, rank, own_acc, own_sum, back, picked, out):
    requests = rank.shape[0]
    kv_heads = picked[0].shape[1] // (2 * LANES)
    ends = [0, picked[0].shape[0], picked[0].shape[0] + picked[1].shape[0]]
    longs = pair_slot.shape[1]
    per_item = own_acc.shape[0] // longs
    heads = per_item // tree

    def kernel(
        pair_ref, rank_ref, acc_ref, sum_ref, back_ref, first, second, _, out_ref, accepted, staged, every, sem
    ):
        sent = []
        for j in range(longs):
            there = slice(j * per_item, (j + 1) * per_item)
            total = jnp.sum(sum_ref[there, :], 1, keepdims=True)
            total = total + back_ref[there, LANES : 2 * LANES].astype(F32)
            whole = acc_ref[there, :] + back_ref[there, :LANES].astype(F32)
            lay(staged.at[j], whole / total, tree)
            sent.append(send_out(j, pair_ref[0, j], staged, out_ref, sem, tree))
        every[ends[0] : ends[1], :] = first[...]
        every[ends[1] : ends[2], :] = second[...]
        for r in range(requests):
            path = every[pl.ds(aligned(rank_ref[r], 16), 16), :]
            for g in range(kv_heads):
                accepted[r * ACCEPT : (r + 1) * ACCEPT, g, :] = path[
                    :ACCEPT, 2 * g * LANES : 2 * (g + 1) * LANES
                ]
        for copy in sent:
            copy.wait()

    return pl.pallas_call(
        kernel,
        out_shape=[
            pltpu.HBM(out.shape, BF16),
            shape((requests * ACCEPT, kv_heads, 2 * LANES), BF16),
        ],
        in_specs=[SMEM] * 2 + [VMEM] * 5 + [ANY],
        out_specs=[ANY, VMEM],
        scratch_shapes=[
            pltpu.VMEM((longs, tree, heads * LANES), BF16),
            pltpu.VMEM((ends[2], picked[0].shape[1]), BF16),
            pltpu.SemaphoreType.DMA((longs,)),
        ],
        input_output_aliases={7: 0},
        compiler_params=params(4),
        cost_estimate=estimate(1),
        name="merge",
    )(pair_slot, rank, own_acc, own_sum, back, *picked, hbm(out))


def swap(value, axis, mask):
    pairs = [(source, source ^ mask) for source in range(lax.axis_size(axis))]
    return lax.ppermute(value, axis, pairs)


def body(
    hidden,
    norm_gain,
    q_weight,
    k_weight,
    v_weight,
    kv_pages,
    page_table,
    cache_len,
    tree_parent,
    accept_node,
    pair_slot,
    far_len,
    far_table,
    mig_src,
    mig_page,
):
    requests, tree = tree_parent.shape
    token_rows = hidden.shape[0]
    own_pages, page_size, kv_heads, entry = kv_pages.shape
    groups = lax.axis_size("grp")
    me = lax.axis_index("grp")
    spot = lax.axis_index("tp")
    counts = chunk_counts(requests)
    firsts = [sum(counts[:c]) for c in range(len(counts))]
    places = [list(range(f, f + n)) for f, n in zip(firsts, counts, strict=True)]

    order, rank, asked, placed, *rows = order_rows(
        hidden, pair_slot, cache_len, mig_src, mig_page, own_pages, groups, tree, counts
    )
    hidden_core = swap(hidden, "tp", 1)
    from_x = [swap(part, "tp", 2) for part in rows]

    migrations = mig_src.shape[0]
    index = jnp.arange(migrations, dtype=I32)
    wanted = lax.all_to_all(asked, "grp", 0, 0, tiled=True)
    outgoing = pick_pages(kv_pages, wanted)
    outgoing, from_x[0] = lax.optimization_barrier((outgoing, from_x[0]))
    from_xc = [swap(part, "tp", 1) for part in from_x]
    incoming = lax.all_to_all(outgoing, "grp", 0, 0, tiled=True)
    moved = incoming.reshape(groups * CAP * page_size, kv_heads * entry)
    held, _ = lax.optimization_barrier((kv_pages, outgoing))
    pool = held.reshape(own_pages * page_size, kv_heads * entry)
    tables = jnp.concatenate([page_table, far_table], 0)
    extra = tables[:, :, None] - own_pages == index[None, None, :]
    tables = jnp.where(
        tables < own_pages, tables, jnp.sum(jnp.where(extra, placed[None, None, :], 0), -1)
    ).reshape(-1)

    parents = tree_parent.reshape(-1, 1)
    half = LANES // 2
    angles = jnp.exp(-THETA_LOG * 2.0 * jnp.arange(half, dtype=F32) / LANES)
    angles = jnp.concatenate([angles, angles])[None, :]
    gain = norm_gain.reshape(-1, hidden.shape[1])
    info = jnp.full((1,), spot, I32)
    far_mine = lax.dynamic_index_in_dim(far_len, me, 0, keepdims=False)
    far_other = lax.dynamic_index_in_dim(far_len, me ^ 1, 0, keepdims=False)

    weights = (q_weight, k_weight, v_weight)
    longs = pair_slot.shape[1]
    scalars = (info, order, rank, cache_len, pair_slot, far_mine, accept_node)
    tables_in = (parents, angles, gain)
    *state, picked0, long_queries = project_first(
        places[0],
        tree,
        longs,
        scalars,
        tables_in,
        weights,
        (hidden, hidden_core, from_x[0], from_xc[0]),
    )
    far_queries = swap(long_queries, "grp", 1)
    out, long_acc, long_sum, far_done = attend_first(
        places[0],
        tree,
        longs,
        requests,
        scalars[1:5],
        far_other,
        tables,
        state,
        far_queries,
        pool,
        moved,
        page_size,
        token_rows,
    )
    back = swap(far_done, "grp", 1)
    out, picked1 = finish(
        places[1],
        tree,
        longs,
        requests,
        scalars,
        tables_in,
        weights,
        (hidden, hidden_core, from_x[1], from_xc[1]),
        tables,
        pool,
        moved,
        page_size,
        out,
    )
    out, accepted = merge(
        tree, pair_slot, rank, long_acc, long_sum, back, (picked0, picked1), out
    )
    return (out, accepted)


def chunk_counts(requests):
    return (requests // 4, requests - requests // 4)


def solution(mesh):
    in_specs = (
        P("grp", "tp"),
        P(),
        P(None, "tp"),
        P(None, "tp"),
        P(None, "tp"),
        P("grp", None, "tp", None),
        P("grp", None),
        P("grp"),
        P("grp", None),
        P("grp"),
        P("grp", None),
        P(),
        P("grp", None),
        P("grp"),
        P("grp"),
    )
    out_specs = (P("grp", "tp"), P("grp", "tp", None))
    chosen = body if mesh.shape["tp"] == 4 else general_body
    return jax.shard_map(chosen, mesh=mesh, in_specs=in_specs, out_specs=out_specs, check_vma=False)
```
